512 devices in a mesh: dp: 32 (over z, x), ctx: 16 (over y, core).
Axes of the slice: x: 4, y: 8, z: 8, core: 2. Of those that a mesh axis runs over, the one named last changes fastest.
Arguments:
- queries: bfloat16 [65536, 16, 128], P(('dp', 'ctx')), may hold values from -700 to 700
- keys: bfloat16 [65536, 4, 128], P(('dp', 'ctx')), may hold values from -6 to 6
- values: bfloat16 [65536, 4, 128], P(('dp', 'ctx')), may hold values from -6 to 6
- out_grad: bfloat16 [65536, 16, 128], P(('dp', 'ctx')), may hold values from -6 to 6
- lengths: int32 [341], replicated, may hold values from 1 to 384, 65536 in all
Outputs:
- query_grad: bfloat16 [65536, 16, 128], P(('dp', 'ctx'))
- key_grad: bfloat16 [65536, 4, 128], P(('dp', 'ctx'))
- value_grad: bfloat16 [65536, 4, 128], P(('dp', 'ctx'))
The draws below stay inside these ranges and needn't reach their ends.
Inputs may be any that keep to these rules, and one draw needn't show every extreme that they name: The lengths add up to 65536; the longest is exactly 384.
All inputs are finite; a program needn't handle non-finite values.
Results may differ from the reference program's by a relative error of at most 0.018.
Values may be sent and summed in bfloat16 or wider, within the bound.
No kernel may reach another device: no remote copies, remote signals or barrier semaphores. Data moves between devices by JAX's collectives and lax.ppermute only.
A program may use at most 64 MiB of HBM per device.

```python
import math
import jax
import jax.numpy as jnp
import numpy as np
from jax import lax

H = 16
KVH = 4
HD = 128
DOCMAX = 384
TOK_DEV = 128
NTOT = 65536
DOCS = 341
REACH = 3


def draw_queries(key, part):
    key = jax.random.fold_in(key, 11)
    base = jax.random.truncated_normal(key, -6.0, 6.0, (NTOT, H, HD), jnp.float32)
    return base.astype(jnp.bfloat16)


def block_scale(stream_key, extent, pieces, least, top_value):
    def one(dim, parts):
        steps = jax.random.uniform(jax.random.fold_in(jax.random.fold_in(stream_key, 6), dim), (parts,), jnp.float32, least / len(pieces), top_value / len(pieces))
        return jnp.repeat(jnp.exp(steps), extent[dim] // parts).reshape((-1,) + (1,) * (len(extent) - dim - 1))

    factor_of = one(*pieces[0])
    for cut in pieces[1:]:
        factor_of = factor_of * one(*cut)
    return factor_of


def split_up(count, total, bound, slope):
    loads = [(1 << 20) // math.isqrt(standing ** slope) + 1 for standing in range(2, count + 1)]
    rest, counts = total - bound - (count - 1), [1] * (count - 1)
    while rest > 0:
        free = [i for i in range(count - 1) if counts[i] < bound]
        pool, remaining = sum([loads[i] for i in free]), rest
        for i in free:
            extra = min(bound - counts[i], max(1, remaining * loads[i] // pool), rest)
            counts[i] = counts[i] + extra
            rest = rest - extra
    return np.array([bound] + counts)


def uneven(own_key, count, total, bound, skew):
    if count == 2:
        one = jax.random.randint(own_key, (), max(1, total - bound), min(bound, total - 1) + 1)
        return jnp.stack([one, total - one])
    sizes = jnp.asarray(split_up(count, total, bound, skew), jnp.int32)
    twos = (count - 1) // 2
    source_of, taker = sizes[1:1 + 2 * twos:2], sizes[2:2 + 2 * twos:2]
    room = jnp.minimum(source_of - 1, bound - taker)
    moved = jax.random.randint(jax.random.fold_in(own_key, 1), (twos,), 0, 1 << 20) % (room + 1)
    sizes = sizes.at[1:1 + 2 * twos:2].set(source_of - moved).at[2:2 + 2 * twos:2].set(taker + moved)
    return sizes[jax.random.permutation(jax.random.fold_in(own_key, 2), count)]


def normal_values(own_key, dims, deviation, bound, pieces=(), held_as=jnp.bfloat16):
    entries = deviation * jax.random.normal(own_key, dims, jnp.float32)
    if pieces:
        entries = entries * block_scale(own_key, dims, pieces, -0.22, 0.18)
    return jnp.clip(entries, -bound, bound).astype(held_as)


def setup_inputs(seed: int = 0) -> dict:
    splits = jax.random.split(jax.random.key(seed), 6)
    queries = draw_queries(jax.random.fold_in(splits[5], 71), 0)
    keys = normal_values(splits[1], (NTOT, KVH, HD), 1.0, 6.0, ((0, 512),))
    values = normal_values(splits[2], (NTOT, KVH, HD), 1.0, 6.0, ((0, 512),))
    out_grad = normal_values(splits[3], (NTOT, H, HD), 1.0, 6.0, ((0, 512),))
    lengths = uneven(splits[4], DOCS, NTOT, DOCMAX, 2).astype(jnp.int32)
    return {"queries": queries, "keys": keys, "values": values, "out_grad": out_grad, "lengths": lengths}


def doc_of(ends, positions):
    return jnp.sum((positions[:, None] >= ends[None, :]).astype(jnp.int32), axis=1).astype(jnp.int32)


def attend_back(items):
    query_blk, key_win, value_win, grad_blk, doc_query, doc_key, pos_query, pos_key = items
    scale = 1.0 / (query_blk.shape[-1] ** 0.5)
    query_f = query_blk.astype(jnp.float32)
    key_f = key_win.astype(jnp.float32)
    value_f = value_win.astype(jnp.float32)
    grad_f = grad_blk.astype(jnp.float32)
    allowed = (doc_query[:, None] == doc_key[None, :]) & (pos_key[None, :] <= pos_query[:, None]) & (pos_key[None, :] >= 0)
    scores = jnp.einsum('qhgd,khd->hgqk', query_f, key_f) * scale
    scores = jnp.where(allowed, scores, -1e30)
    top = jnp.max(scores, axis=-1, keepdims=True)
    expo = jnp.where(allowed, jnp.exp(scores - top), 0.0)
    probs = expo / jnp.sum(expo, axis=-1, keepdims=True)
    probs_low = probs.astype(jnp.bfloat16).astype(jnp.float32)
    attn_out = jnp.einsum('hgqk,khd->qhgd', probs_low, value_f)
    delta = jnp.sum(grad_f * attn_out, axis=-1)
    prob_grad = jnp.einsum('qhgd,khd->hgqk', grad_f, value_f)
    score_grad = probs * (prob_grad - jnp.transpose(delta, (1, 2, 0))[..., None]) * scale
    score_low = score_grad.astype(jnp.bfloat16).astype(jnp.float32)
    query_grad = jnp.einsum('hgqk,khd->qhgd', score_low, key_f).astype(jnp.bfloat16)
    key_part = jnp.einsum('hgqk,qhgd->khd', score_low, query_f)
    value_part = jnp.einsum('hgqk,qhgd->khd', probs_low, grad_f)
    return query_grad, key_part, value_part


def reference(queries, keys, values, out_grad, lengths):
    rows = TOK_DEV
    lead = REACH * rows
    width = lead + rows
    total, heads, head_dim = queries.shape
    kv_heads = keys.shape[1]
    group = heads // kv_heads
    blocks = total // rows
    ends = jnp.cumsum(lengths).astype(jnp.int32)
    padding = ((lead, 0), (0, 0), (0, 0))
    key_pad = jnp.pad(keys, padding)
    value_pad = jnp.pad(values, padding)
    query_b = queries.reshape(blocks, rows, kv_heads, group, head_dim)
    grad_b = out_grad.reshape(blocks, rows, kv_heads, group, head_dim)

    def advance(carry, items):
        key_acc, value_acc = carry
        index, query_blk, grad_blk = items
        begin = (index * rows).astype(jnp.int32)
        key_win = lax.dynamic_slice_in_dim(key_pad, begin, width, 0)
        value_win = lax.dynamic_slice_in_dim(value_pad, begin, width, 0)
        pos_query = (begin + jnp.arange(rows, dtype=jnp.int32)).astype(jnp.int32)
        pos_key = (begin - lead + jnp.arange(width, dtype=jnp.int32)).astype(jnp.int32)
        doc_query = doc_of(ends, pos_query)
        doc_key = doc_of(ends, pos_key)
        query_grad, key_part, value_part = attend_back((query_blk, key_win, value_win, grad_blk, doc_query, doc_key, pos_query, pos_key))
        key_acc = lax.dynamic_update_slice_in_dim(key_acc, lax.dynamic_slice_in_dim(key_acc, begin, width, 0) + key_part, begin, 0)
        value_acc = lax.dynamic_update_slice_in_dim(value_acc, lax.dynamic_slice_in_dim(value_acc, begin, width, 0) + value_part, begin, 0)
        return (key_acc, value_acc), query_grad

    empty = jnp.zeros((total + lead, kv_heads, head_dim), jnp.float32)
    index = jnp.arange(blocks, dtype=jnp.int32)
    (key_acc, value_acc), query_grad = lax.scan(advance, (empty, empty), (index, query_b, grad_b))
    return (query_grad.reshape(total, heads, head_dim),
            key_acc[lead:].astype(jnp.bfloat16),
            value_acc[lead:].astype(jnp.bfloat16))
```

```python
import jax
import jax.numpy as jnp
from jax import lax
from jax.experimental import pallas as pl
from jax.experimental.pallas import tpu as pltpu
from jax.sharding import PartitionSpec as P

AXES = ("dp", "ctx")
BF = jnp.bfloat16
F32 = jnp.float32
VMEM = 48 * 1024 * 1024
NT = (((1,), (1,)), ((), ()))
TN = (((0,), (0,)), ((), ()))


def hot(rows, cols, source):
    o = lax.broadcasted_iota(jnp.int32, (rows, cols), 0)
    r = lax.broadcasted_iota(jnp.int32, (rows, cols), 1)
    return jnp.where(r == source(o), 1.0, 0.0).astype(BF)


def pick(onehot, block):
    return jnp.dot(onehot, block, preferred_element_type=F32).astype(BF)


def split_heads(place_ref, len_ref, q_ref, g_ref, qs_ref, gs_ref, low_ref):
    heads, rows, _ = qs_ref.shape
    n_docs = len_ref.shape[1]
    step = 256 // heads
    turn = hot(256, 256, lambda o: lax.rem(o, step) * heads + o // step)
    for src, dst in ((q_ref, qs_ref), (g_ref, gs_ref)):
        for ch in range(rows // step):
            got = pick(turn, src[ch * 256 : (ch + 1) * 256, :])
            for h in range(heads):
                dst[h, ch * step : (ch + 1) * step, :] = got[h * step : (h + 1) * step, :]
    start = place_ref[0]
    group_rows = low_ref.shape[1]
    i = lax.broadcasted_iota(jnp.int32, (n_docs, n_docs), 1)
    j = lax.broadcasted_iota(jnp.int32, (n_docs, n_docs), 0)
    ends = jnp.sum(jnp.where(i <= j, len_ref[...], 0), axis=1, keepdims=True)
    pos = start + lax.rem(lax.broadcasted_iota(jnp.int32, (1, group_rows), 1), rows)
    first = jnp.max(jnp.where(ends <= pos, ends, 0), axis=0, keepdims=True)
    low_ref[...] = jnp.broadcast_to(first - (start - 3 * rows), low_ref.shape)


def attend(place_ref, low_ref, qs_ref, gs_ref, share_ref, far_ref, own_ref,
           ps_ref, ds_ref, kw_ref, near_ref, cross_ref, base_ref, kv_win, parts):
    j = pl.program_id(0)
    core = place_ref[1]
    rows = near_ref.shape[2]
    kv_heads = kv_win.shape[1]
    tok = 256 // kv_heads
    scale = 1.0 / qs_ref.shape[-1] ** 0.5

    @pl.when(j == 0)
    def _():
        turn = hot(256, 256, lambda o: lax.rem(o, tok) * kv_heads + o // tok)

        def fill(block, load):
            for s in range(2):
                for ch in range(rows // tok):
                    got = pick(turn, load(s, ch * 256))
                    at = pl.ds(pl.multiple_of(block * rows + ch * tok, tok), tok)
                    for h in range(kv_heads):
                        kv_win[s, h, at, :] = got[h * tok : (h + 1) * tok, :]

        fill(3, lambda s, r: own_ref[s, r : r + 256, :])
        fill(1, lambda s, r: share_ref[core, s, r : r + 256, :])
        fill(2 - 2 * core, lambda s, r: share_ref[1 - core, s, r : r + 256, :])
        fill(2 * core, lambda s, r: far_ref[s, r : r + 256, :])

    keys, vals = kv_win[0, j], kv_win[1, j]
    kw_ref[0] = keys
    q, g = qs_ref[0], gs_ref[0]
    width, n_rows = keys.shape[0], q.shape[0]
    chunk = 256
    for c in range(n_rows // chunk):
        cols = slice(c * chunk, (c + 1) * chunk)
        kp = lax.broadcasted_iota(jnp.int32, (width, chunk), 0)
        tq = lax.rem(lax.broadcasted_iota(jnp.int32, (1, chunk), 1) + c * chunk, rows) + 3 * rows
        allowed = (kp >= low_ref[0:1, cols]) & (kp <= tq)
        s = lax.dot_general(keys, q[cols, :], NT, preferred_element_type=F32)
        s = jnp.where(allowed, s, -1e30)
        top = jnp.max(s, axis=0, keepdims=True)
        e = jnp.exp2((s - top) * (scale * 1.4426950408889634))
        p = e * (1.0 / jnp.sum(e, axis=0, keepdims=True))
        ps_ref[0, :, cols] = p.astype(BF)
        dp = lax.dot_general(vals, g[cols, :], NT, preferred_element_type=F32)
        delta = jnp.sum(p * dp, axis=0, keepdims=True)
        ds_ref[0, :, cols] = (p * scale * (dp - delta)).astype(BF)
    lead = 3 * rows
    parts[0] = jnp.dot(ds_ref[0, :lead, :], q, preferred_element_type=F32).astype(BF)
    parts[1] = jnp.dot(ps_ref[0, :lead, :], g, preferred_element_type=F32).astype(BF)
    for s in range(2):
        base_ref[s, j] = parts[s, rows : 2 * rows, :]
        near_ref[s, j] = parts[s, pl.ds(pl.multiple_of(2 * core * rows, rows), rows), :]
        cross_ref[s, j] = parts[s, pl.ds(pl.multiple_of((2 - 2 * core) * rows, rows), rows), :]


def local_grads(ps_ref, ds_ref, kw_ref, qs_ref, gs_ref, dq_ref, loc_ref, dq_all):
    j = pl.program_id(0)
    heads, rows, _ = dq_all.shape
    group = qs_ref.shape[1] // rows
    ds = ds_ref[0]
    dq_t = lax.dot_general(kw_ref[0], ds, TN, preferred_element_type=F32)
    for x in range(group):
        dq_all[j * group + x] = dq_t[:, x * rows : (x + 1) * rows].T.astype(BF)
    lead = 3 * rows
    loc_ref[0, 0] = jnp.dot(ds[lead:, :], qs_ref[0], preferred_element_type=F32)
    loc_ref[1, 0] = jnp.dot(ps_ref[0, lead:, :], gs_ref[0], preferred_element_type=F32)

    @pl.when(j == pl.num_programs(0) - 1)
    def _():
        step = 256 // heads
        turn = hot(256, 256, lambda o: lax.rem(o, heads) * step + o // heads)
        for ch in range(rows // step):
            block = dq_all[:, ch * step : (ch + 1) * step, :].reshape(256, -1)
            dq_ref[ch * 256 : (ch + 1) * 256, :] = pick(turn, block)


def finish(place_ref, loc_ref, a_ref, b_ref, near_ref, dk_ref, dv_ref):
    _, kv_heads, rows, _ = loc_ref.shape
    tok = 256 // kv_heads
    turn = hot(256, 256, lambda o: lax.rem(o, kv_heads) * tok + o // kv_heads)
    mine = jnp.where(place_ref[1] == 0, 1.0, 0.0)
    for s, out in ((0, dk_ref), (1, dv_ref)):
        for ch in range(rows // tok):
            at = (s, slice(None), slice(ch * tok, (ch + 1) * tok), slice(None))
            total = loc_ref[at] + a_ref[at].astype(F32) + b_ref[at].astype(F32)
            total = total + near_ref[at].astype(F32) * mine
            out[ch * 256 : (ch + 1) * 256, :] = pick(turn, total.astype(BF).reshape(256, -1))


def body(queries, keys, values, out_grad, lengths):
    rows, heads, dim = queries.shape
    kv_heads = keys.shape[1]
    group = heads // kv_heads
    width = 4 * rows
    n_ctx = lax.axis_size("ctx")
    n = lax.axis_size("dp") * n_ctx
    core = lax.rem(lax.axis_index("ctx"), 2)
    place = jnp.stack([lax.axis_index(AXES) * rows, core]).astype(jnp.int32)

    def send(block, distance, cores=(0, 1)):
        route = [(i, i + distance) for i in range(n) if i % 2 in cores and 0 <= i + distance < n]
        return lax.ppermute(block, AXES, route)

    smem = pl.BlockSpec(memory_space=pltpu.SMEM)
    params = pltpu.CompilerParams(vmem_limit_bytes=VMEM)
    q_flat, g_flat = queries.reshape(rows * heads, dim), out_grad.reshape(rows * heads, dim)
    own = jnp.stack([keys.reshape(rows * kv_heads, dim), values.reshape(rows * kv_heads, dim)])

    got = send(own, 2, (1,)), send(own, 2, (0,))
    far = send(jnp.where(core == 0, own, got[0]), 1)
    pairs = [[2 * i, 2 * i + 1] for i in range(n_ctx // 2)]
    share = lax.all_gather(jnp.where(core == 0, got[1], got[0]), "ctx", axis_index_groups=pairs)

    qs, gs, low = pl.pallas_call(
        split_heads,
        in_specs=[smem] + [pl.BlockSpec(memory_space=pltpu.VMEM)] * 3,
        out_shape=[jax.ShapeDtypeStruct((heads, rows, dim), BF)] * 2
        + [jax.ShapeDtypeStruct((8, group * rows), jnp.int32)],
        compiler_params=params,
        cost_estimate=pl.CostEstimate(flops=300_000_000, bytes_accessed=2_000_000, transcendentals=0),
        name="split_heads",
    )(place, lengths.reshape(1, -1), q_flat, g_flat)
    qs = qs.reshape(kv_heads, group * rows, dim)
    gs = gs.reshape(kv_heads, group * rows, dim)

    per_head = lambda *shape: pl.BlockSpec((1,) + shape, lambda j: (j, 0, 0))
    whole = lambda *shape: pl.BlockSpec(shape, lambda j: (0,) * len(shape))
    sums = (2, kv_heads, rows, dim)
    ps, ds, kw, near, cross, base = pl.pallas_call(
        attend,
        grid=(kv_heads,),
        in_specs=[
            smem,
            whole(8, group * rows),
            per_head(group * rows, dim),
            per_head(group * rows, dim),
            whole(2, 2, rows * kv_heads, dim),
            whole(2, rows * kv_heads, dim),
            whole(2, rows * kv_heads, dim),
        ],
        out_specs=[per_head(width, group * rows)] * 2 + [per_head(width, dim)] + [whole(*sums)] * 3,
        out_shape=[jax.ShapeDtypeStruct((kv_heads, width, group * rows), BF)] * 2
        + [jax.ShapeDtypeStruct((kv_heads, width, dim), BF)]
        + [jax.ShapeDtypeStruct(sums, BF)] * 3,
        scratch_shapes=[
            pltpu.VMEM((2, kv_heads, width, dim), BF),
            pltpu.VMEM((2, 3 * rows, dim), BF),
        ],
        compiler_params=params,
        cost_estimate=pl.CostEstimate(flops=1_200_000_000, bytes_accessed=8_000_000, transcendentals=1 << 20),
        name="attend",
    )(place, low, qs, gs, share, far, own)

    near_got = send(near, -1)
    cross_got = send(cross, 0) if n == 1 else lax.ppermute(cross, AXES, [(i, i ^ 1) for i in range(n)])
    part = base.astype(F32) + cross_got.astype(F32)
    back_0 = send(part.astype(BF), -2, (0,))
    back_1 = send((part + near_got.astype(F32)).astype(BF), -2, (1,))

    dq, loc = pl.pallas_call(
        local_grads,
        grid=(kv_heads,),
        in_specs=[
            per_head(width, group * rows),
            per_head(width, group * rows),
            per_head(width, dim),
            per_head(group * rows, dim),
            per_head(group * rows, dim),
        ],
        out_specs=[
            whole(rows * heads, dim),
            pl.BlockSpec((2, 1, rows, dim), lambda j: (0, j, 0, 0)),
        ],
        out_shape=[
            jax.ShapeDtypeStruct((rows * heads, dim), BF),
            jax.ShapeDtypeStruct(sums, F32),
        ],
        scratch_shapes=[pltpu.VMEM((heads, rows, dim), BF)],
        compiler_params=params,
        cost_estimate=pl.CostEstimate(flops=500_000_000, bytes_accessed=8_000_000, transcendentals=0),
        name="local_grads",
    )(ps, ds, kw, qs, gs)

    vmem = pl.BlockSpec(memory_space=pltpu.VMEM)
    dk, dv = pl.pallas_call(
        finish,
        in_specs=[smem] + [vmem] * 4,
        out_shape=[jax.ShapeDtypeStruct((rows * kv_heads, dim), BF)] * 2,
        compiler_params=params,
        name="finish",
    )(place, loc, back_0, back_1, near_got)
    return (
        dq.reshape(rows, heads, dim),
        dk.reshape(rows, kv_heads, dim),
        dv.reshape(rows, kv_heads, dim),
    )


def solution(mesh):
    token = P(AXES, None, None)
    return jax.shard_map(
        body,
        mesh=mesh,
        in_specs=(token, token, token, token, P()),
        out_specs=(token, token, token),
        check_vma=False,
    )
```

```python
import jax
import jax.numpy as jnp
from jax import lax
from jax.experimental import pallas as pl
from jax.experimental.pallas import tpu as pltpu
from jax.sharding import PartitionSpec as P

AXES = ("dp", "ctx")
BF = jnp.bfloat16
F32 = jnp.float32
VMEM = 28 * 1024 * 1024
NT = (((1,), (1,)), ((), ()))
TN = (((0,), (0,)), ((), ()))
LOG2E = 1.4426950408889634
PARAMS = pltpu.CompilerParams(vmem_limit_bytes=VMEM)
IN_VMEM = pl.BlockSpec(memory_space=pltpu.VMEM)
IN_SMEM = pl.BlockSpec(memory_space=pltpu.SMEM)
IN_HBM = pl.BlockSpec(memory_space=pltpu.HBM)


def hot(source):
    o = lax.broadcasted_iota(jnp.int32, (256, 256), 0)
    r = lax.broadcasted_iota(jnp.int32, (256, 256), 1)
    return jnp.where(r == source(o), 1.0, 0.0).astype(BF)


def pick(onehot, block):
    return jnp.dot(onehot, block, preferred_element_type=F32).astype(BF)


def to_heads(heads):
    step = 256 // heads
    return hot(lambda o: lax.rem(o, step) * heads + o // step)


def to_tokens(heads):
    step = 256 // heads
    return hot(lambda o: lax.rem(o, heads) * step + o // heads)


def pack(k_ref, v_ref, own_ref, k_buf, v_buf, sems):
    copies = [pltpu.make_async_copy(src, dst, sems.at[i]) for i, (src, dst) in enumerate(((k_ref, k_buf), (v_ref, v_buf)))]
    for copy in copies:
        copy.start()
    _, heads, rows, _ = own_ref.shape
    step = 256 // heads
    turn = to_heads(heads)
    for s, buf in enumerate((k_buf, v_buf)):
        copies[s].wait()
        for ch in range(rows // step):
            got = pick(turn, buf[ch * 256 : (ch + 1) * 256, :])
            for h in range(heads):
                own_ref[s, h, ch * step : (ch + 1) * step, :] = got[h * step : (h + 1) * step, :]


def diagonal(low, rows, n_rows):
    kp = lax.broadcasted_iota(jnp.int32, (rows, n_rows), 0)
    tq = lax.rem(lax.broadcasted_iota(jnp.int32, (1, n_rows), 1), rows)
    return (kp + 3 * rows >= low) & (kp <= tq)


def prepare(place_ref, len_ref, q_ref, g_ref, own_ref, qs_ref, gs_ref, low_ref, stat_ref, q_buf, g_buf, sems):
    copies = [pltpu.make_async_copy(src, dst, sems.at[i]) for i, (src, dst) in enumerate(((q_ref, q_buf), (g_ref, g_buf)))]
    for copy in copies:
        copy.start()
    kv_heads, n_rows, dim = qs_ref.shape
    rows = own_ref.shape[2]
    group = n_rows // rows
    heads = kv_heads * group
    n_docs = len_ref.shape[1]
    step = 256 // heads
    turn = to_heads(heads)
    start = place_ref[0]
    i = lax.broadcasted_iota(jnp.int32, (n_docs, n_docs), 1)
    j = lax.broadcasted_iota(jnp.int32, (n_docs, n_docs), 0)
    ends = jnp.sum(jnp.where(i <= j, len_ref[...], 0), axis=1, keepdims=True)
    pos = start + lax.rem(lax.broadcasted_iota(jnp.int32, (1, n_rows), 1), rows)
    first = jnp.max(jnp.where(ends <= pos, ends, 0), axis=0, keepdims=True)
    low = first - (start - 3 * rows)
    low_ref[...] = jnp.broadcast_to(low, low_ref.shape)
    for s, (buf, dst) in enumerate(((q_buf, qs_ref), (g_buf, gs_ref))):
        copies[s].wait()
        for ch in range(rows // step):
            got = pick(turn, buf[ch * 256 : (ch + 1) * 256, :])
            for h in range(heads):
                at = (h % group) * rows + ch * step
                dst[h // group, at : at + step, :] = got[h * step : (h + 1) * step, :]
    allowed = diagonal(low, rows, n_rows)
    for h in range(kv_heads):
        s = lax.dot_general(own_ref[0, h], qs_ref[h], NT, preferred_element_type=F32)
        dp = lax.dot_general(own_ref[1, h], gs_ref[h], NT, preferred_element_type=F32)
        s = jnp.where(allowed, s, -1e30)
        top = jnp.max(s, axis=0, keepdims=True)
        e = jnp.exp2((s - top) * (LOG2E / dim**0.5))
        stat_ref[h, 0:1, :] = top
        stat_ref[h, 1:2, :] = jnp.sum(e, axis=0, keepdims=True)
        stat_ref[h, 2:3, :] = jnp.sum(e * dp, axis=0, keepdims=True)


def attend(place_ref, low_ref, stat_ref, qs_ref, gs_ref, far_ref, first_ref, got_ref, other_ref,
           ds_ref, kw_ref, final_ref, away_ref, cross_ref, base_ref, ps_buf, vw_buf):
    kv_heads, n_rows, dim = qs_ref.shape
    rows = got_ref.shape[2]
    even = place_ref[1] == 0
    scale = 1.0 / dim**0.5
    lead = 3 * rows
    chunk = 256

    def soft(h):
        for s, win in ((0, kw_ref.at[h]), (1, vw_buf.at[h])):
            win[:rows, :] = jnp.where(even, far_ref[s, h], other_ref[s, h])
            win[rows : 2 * rows, :] = got_ref[s, h]
            win[2 * rows :, :] = jnp.where(even, other_ref[s, h], first_ref[s, h])
        for c in range(n_rows // chunk):
            cols = slice(c * chunk, (c + 1) * chunk)
            s = lax.dot_general(kw_ref[h], qs_ref[h, cols, :], NT, preferred_element_type=F32)
            dp = lax.dot_general(vw_buf[h], gs_ref[h, cols, :], NT, preferred_element_type=F32)
            kp = lax.broadcasted_iota(jnp.int32, (lead, chunk), 0)
            s = jnp.where(kp >= low_ref[0:1, cols], s, -1e30)
            old = stat_ref[h, 0:1, cols]
            top = jnp.maximum(jnp.max(s, axis=0, keepdims=True), old)
            e = jnp.exp2((s - top) * (scale * LOG2E))
            keep = jnp.exp2((old - top) * (scale * LOG2E))
            r = 1.0 / (jnp.sum(e, axis=0, keepdims=True) + keep * stat_ref[h, 1:2, cols])
            delta = (jnp.sum(e * dp, axis=0, keepdims=True) + keep * stat_ref[h, 2:3, cols]) * r
            final_ref[h, 0:1, cols] = top
            final_ref[h, 1:2, cols] = r
            final_ref[h, 2:3, cols] = delta
            p = e * r
            ps_buf[h, :, cols] = p.astype(BF)
            ds_ref[h, :, cols] = (p * (dp - delta)).astype(BF)

    def sums(h):
        dk = (jnp.dot(ds_ref[h], qs_ref[h], preferred_element_type=F32) * scale).astype(BF)
        dv = jnp.dot(ps_buf[h], gs_ref[h], preferred_element_type=F32).astype(BF)
        for s, x in ((0, dk), (1, dv)):
            base_ref[s, h] = x[rows : 2 * rows]
            away_ref[s, h] = x[:rows]
            cross_ref[0, s, h] = jnp.where(even, x[2 * rows :], x[:rows])
            cross_ref[1, s, h] = x[2 * rows :]

    for h in range(kv_heads):
        soft(h)
        if h:
            sums(h - 1)
    sums(kv_heads - 1)


def own_part(low_ref, final_ref, qs_ref, gs_ref, own_ref, dso_ref, loc_ref):
    kv_heads, n_rows, dim = qs_ref.shape
    rows = own_ref.shape[2]
    scale = 1.0 / dim**0.5
    allowed = diagonal(low_ref[0:1, :], rows, n_rows)
    for h in range(kv_heads):
        s = lax.dot_general(own_ref[0, h], qs_ref[h], NT, preferred_element_type=F32)
        dp = lax.dot_general(own_ref[1, h], gs_ref[h], NT, preferred_element_type=F32)
        s = jnp.where(allowed, s, -1e30)
        p = jnp.exp2((s - final_ref[h, 0:1, :]) * (scale * LOG2E)) * final_ref[h, 1:2, :]
        ds = (p * (dp - final_ref[h, 2:3, :])).astype(BF)
        dso_ref[h] = ds
        loc_ref[0, h] = jnp.dot(ds, qs_ref[h], preferred_element_type=F32) * scale
        loc_ref[1, h] = jnp.dot(p.astype(BF), gs_ref[h], preferred_element_type=F32)


def query_part(ds_ref, kw_ref, dso_ref, own_ref, dq_ref, dq_all, out_buf, sems):
    kv_heads, _, n_rows = ds_ref.shape
    rows, dim = own_ref.shape[2:]
    group = n_rows // rows
    heads = kv_heads * group
    step = 256 // heads
    scale = 1.0 / dim**0.5
    for h in range(kv_heads):
        dq = lax.dot_general(kw_ref[h], ds_ref[h], TN, preferred_element_type=F32)
        dq = (dq + lax.dot_general(own_ref[0, h], dso_ref[h], TN, preferred_element_type=F32)) * scale
        for x in range(group):
            dq_all[h * group + x] = dq[:, x * rows : (x + 1) * rows].T.astype(BF)
    turn = to_tokens(heads)
    copies = []
    half = rows * heads // 2
    for ch in range(rows // step):
        block = dq_all[:, ch * step : (ch + 1) * step, :].reshape(256, dim)
        out_buf[ch * 256 : (ch + 1) * 256, :] = pick(turn, block)
        if (ch + 1) * 256 % half == 0:
            at = pl.ds(len(copies) * half, half)
            copies.append(pltpu.make_async_copy(out_buf.at[at, :], dq_ref.at[at, :], sems.at[len(copies)]))
            copies[-1].start()
    for copy in copies:
        copy.wait()


def finish(place_ref, loc_ref, back_ref, away_ref, cross_ref, dk_ref, dv_ref, buf, sems):
    _, kv_heads, rows, dim = loc_ref.shape
    tok = 256 // kv_heads
    turn = to_tokens(kv_heads)
    mine = jnp.where(place_ref[1] == 0, 1.0, 0.0)
    copies = []
    for s, out in ((0, dk_ref), (1, dv_ref)):
        for ch in range(rows // tok):
            at = (s, slice(None), slice(ch * tok, (ch + 1) * tok), slice(None))
            total = loc_ref[at] + away_ref[at].astype(F32) + cross_ref[(1,) + at].astype(F32) * mine
            total = total + back_ref[at].astype(F32)
            buf[s, ch * 256 : (ch + 1) * 256, :] = pick(turn, total.astype(BF).reshape(256, dim))
        copies.append(pltpu.make_async_copy(buf.at[s], out, sems.at[s]))
        copies[-1].start()
    for copy in copies:
        copy.wait()


def body(queries, keys, values, out_grad, lengths):
    rows, heads, dim = queries.shape
    kv_heads = keys.shape[1]
    n_rows = heads // kv_heads * rows
    lead = 3 * rows
    n = lax.axis_size("dp") * lax.axis_size("ctx")
    core = lax.rem(lax.axis_index("ctx"), 2)
    place = jnp.stack([lax.axis_index(AXES) * rows, core]).astype(jnp.int32)
    shape = jax.ShapeDtypeStruct
    sums = (2, kv_heads, rows, dim)

    def send(block, distance, cores=(0, 1)):
        route = [(i, i + distance) for i in range(n) if i % 2 in cores and 0 <= i + distance < n]
        return lax.ppermute(block, AXES, route)

    hbm = lambda x: pltpu.with_memory_space_constraint(x, pltpu.HBM)
    own = pl.pallas_call(
        pack,
        in_specs=[IN_HBM] * 2,
        out_shape=shape(sums, BF),
        out_specs=IN_VMEM,
        scratch_shapes=[pltpu.VMEM((rows * kv_heads, dim), BF)] * 2 + [pltpu.SemaphoreType.DMA((2,))],
        compiler_params=PARAMS,
        name="pack",
    )(hbm(keys.reshape(rows * kv_heads, dim)), hbm(values.reshape(rows * kv_heads, dim)))

    got = send(own, 2)
    far = send(own, 3, (1,))
    first = send(own, 1, (0,))
    qs, gs, low, stat = pl.pallas_call(
        prepare,
        in_specs=[IN_SMEM, IN_VMEM, IN_HBM, IN_HBM, IN_VMEM],
        out_shape=[shape((kv_heads, n_rows, dim), BF)] * 2 + [shape((8, n_rows), jnp.int32), shape((kv_heads, 8, n_rows), F32)],
        out_specs=[IN_VMEM] * 4,
        scratch_shapes=[pltpu.VMEM((rows * heads, dim), BF)] * 2 + [pltpu.SemaphoreType.DMA((2,))],
        compiler_params=PARAMS,
        cost_estimate=pl.CostEstimate(flops=1_000_000_000, bytes_accessed=4_000_000, transcendentals=1 << 18),
        name="prepare",
    )(place, lengths.reshape(1, -1), hbm(queries.reshape(rows * heads, dim)), hbm(out_grad.reshape(rows * heads, dim)), own)
    got, qs = lax.optimization_barrier((got, qs))
    other = lax.ppermute(got, AXES, [(i, i ^ 1) for i in range(n)])

    ds, kw, final, away, cross, base = pl.pallas_call(
        attend,
        in_specs=[IN_SMEM] + [IN_VMEM] * 8,
        out_shape=[shape((kv_heads, lead, n_rows), BF), shape((kv_heads, lead, dim), BF), shape((kv_heads, 8, n_rows), F32)]
        + [shape(sums, BF), shape((2,) + sums, BF), shape(sums, BF)],
        out_specs=[IN_VMEM] * 6,
        scratch_shapes=[pltpu.VMEM((kv_heads, lead, n_rows), BF), pltpu.VMEM((kv_heads, lead, dim), BF)],
        compiler_params=PARAMS,
        cost_estimate=pl.CostEstimate(flops=1_000_000_000, bytes_accessed=8_000_000, transcendentals=1 << 20),
        name="attend",
    )(place, low, stat, qs, gs, far, first, got, other)

    cross_got = lax.ppermute(cross, AXES, [(i, i ^ 1) for i in range(n)])
    away_got = send(away, -3, (0,))
    part = (base.astype(F32) + cross_got[0].astype(F32)).astype(BF)
    back = send(part, -2)
    part, final, kw = lax.optimization_barrier((part, final, kw))
    dso, loc = pl.pallas_call(
        own_part,
        in_specs=[IN_VMEM] * 5,
        out_shape=[shape((kv_heads, rows, n_rows), BF), shape(sums, F32)],
        out_specs=[IN_VMEM] * 2,
        compiler_params=PARAMS,
        cost_estimate=pl.CostEstimate(flops=300_000_000, bytes_accessed=4_000_000, transcendentals=1 << 18),
        name="own_part",
    )(low, final, qs, gs, own)
    dq = pl.pallas_call(
        query_part,
        in_specs=[IN_VMEM] * 4,
        out_shape=shape((rows * heads, dim), BF),
        out_specs=IN_HBM,
        scratch_shapes=[pltpu.VMEM((heads, rows, dim), BF), pltpu.VMEM((rows * heads, dim), BF), pltpu.SemaphoreType.DMA((2,))],
        compiler_params=PARAMS,
        cost_estimate=pl.CostEstimate(flops=800_000_000, bytes_accessed=4_000_000, transcendentals=0),
        name="query_part",
    )(ds, kw, dso, own)

    dk, dv = pl.pallas_call(
        finish,
        in_specs=[IN_SMEM] + [IN_VMEM] * 4,
        out_shape=[shape((rows * kv_heads, dim), BF)] * 2,
        out_specs=[IN_HBM] * 2,
        scratch_shapes=[pltpu.VMEM((2, rows * kv_heads, dim), BF), pltpu.SemaphoreType.DMA((2,))],
        compiler_params=PARAMS,
        name="finish",
    )(place, loc, back, away_got, cross_got)
    return dq.reshape(rows, heads, dim), dk.reshape(rows, kv_heads, dim), dv.reshape(rows, kv_heads, dim)


def solution(mesh):
    token = P(AXES, None, None)
    return jax.shard_map(
        body,
        mesh=mesh,
        in_specs=(token, token, token, token, P()),
        out_specs=(token, token, token),
        check_vma=False,
    )
```

```python
import jax
import jax.numpy as jnp
from jax import lax
from jax.experimental import pallas as pl
from jax.experimental.pallas import tpu as pltpu
from jax.sharding import PartitionSpec as P

AXES = ("dp", "ctx")
BF = jnp.bfloat16
F32 = jnp.float32
VMEM = 28 * 1024 * 1024
NT = (((1,), (1,)), ((), ()))
TN = (((0,), (0,)), ((), ()))
LOG2E = 1.4426950408889634
PARAMS = pltpu.CompilerParams(vmem_limit_bytes=VMEM)
IN_VMEM = pl.BlockSpec(memory_space=pltpu.VMEM)
IN_SMEM = pl.BlockSpec(memory_space=pltpu.SMEM)
IN_HBM = pl.BlockSpec(memory_space=pltpu.HBM)


def hot(source):
    o = lax.broadcasted_iota(jnp.int32, (256, 256), 0)
    r = lax.broadcasted_iota(jnp.int32, (256, 256), 1)
    return jnp.where(r == source(o), 1.0, 0.0).astype(BF)


def pick(onehot, block):
    return jnp.dot(onehot, block, preferred_element_type=F32).astype(BF)


def to_heads(heads):
    step = 256 // heads
    return hot(lambda o: lax.rem(o, step) * heads + o // step)


def to_tokens(heads):
    step = 256 // heads
    return hot(lambda o: lax.rem(o, heads) * step + o // heads)


def pack(k_ref, v_ref, own_ref, k_buf, v_buf, sems):
    copies = [pltpu.make_async_copy(src, dst, sems.at[i]) for i, (src, dst) in enumerate(((k_ref, k_buf), (v_ref, v_buf)))]
    for copy in copies:
        copy.start()
    _, heads, rows, _ = own_ref.shape
    step = 256 // heads
    turn = to_heads(heads)
    for s, buf in enumerate((k_buf, v_buf)):
        copies[s].wait()
        for ch in range(rows // step):
            got = pick(turn, buf[ch * 256 : (ch + 1) * 256, :])
            for h in range(heads):
                own_ref[s, h, ch * step : (ch + 1) * step, :] = got[h * step : (h + 1) * step, :]


def diagonal(low, rows, n_rows):
    kp = lax.broadcasted_iota(jnp.int32, (rows, n_rows), 0)
    tq = lax.rem(lax.broadcasted_iota(jnp.int32, (1, n_rows), 1), rows)
    return (kp + 3 * rows >= low) & (kp <= tq)


def prepare(place_ref, len_ref, q_ref, g_ref, own_ref, qs_ref, gs_ref, low_ref, stat_ref, q_buf, g_buf, sems):
    copies = [pltpu.make_async_copy(src, dst, sems.at[i]) for i, (src, dst) in enumerate(((q_ref, q_buf), (g_ref, g_buf)))]
    for copy in copies:
        copy.start()
    kv_heads, n_rows, dim = qs_ref.shape
    rows = own_ref.shape[2]
    group = n_rows // rows
    heads = kv_heads * group
    n_docs = len_ref.shape[1]
    step = 256 // heads
    turn = to_heads(heads)
    start = place_ref[0]
    i = lax.broadcasted_iota(jnp.int32, (n_docs, n_docs), 1)
    j = lax.broadcasted_iota(jnp.int32, (n_docs, n_docs), 0)
    ends = jnp.sum(jnp.where(i <= j, len_ref[...], 0), axis=1, keepdims=True)
    pos = start + lax.rem(lax.broadcasted_iota(jnp.int32, (1, n_rows), 1), rows)
    first = jnp.max(jnp.where(ends <= pos, ends, 0), axis=0, keepdims=True)
    low = first - (start - 3 * rows)
    low_ref[...] = jnp.broadcast_to(low, low_ref.shape)
    for s, (buf, dst) in enumerate(((q_buf, qs_ref), (g_buf, gs_ref))):
        copies[s].wait()
        for ch in range(rows // step):
            got = pick(turn, buf[ch * 256 : (ch + 1) * 256, :])
            for h in range(heads):
                at = (h % group) * rows + ch * step
                dst[h // group, at : at + step, :] = got[h * step : (h + 1) * step, :]
    allowed = diagonal(low, rows, n_rows)
    for h in range(kv_heads):
        s = lax.dot_general(own_ref[0, h], qs_ref[h], NT, preferred_element_type=F32)
        dp = lax.dot_general(own_ref[1, h], gs_ref[h], NT, preferred_element_type=F32)
        s = jnp.where(allowed, s, -1e30)
        top = jnp.max(s, axis=0, keepdims=True)
        e = jnp.exp2((s - top) * (LOG2E / dim**0.5))
        stat_ref[h, 0:1, :] = top
        stat_ref[h, 1:2, :] = jnp.sum(e, axis=0, keepdims=True)
        stat_ref[h, 2:3, :] = jnp.sum(e * dp, axis=0, keepdims=True)


def attend(place_ref, low_ref, stat_ref, qs_ref, gs_ref, side_ref, both_ref,
           ds_ref, kw_ref, final_ref, away_ref, cross_ref, base_ref, ps_buf, vw_buf):
    kv_heads, n_rows, dim = qs_ref.shape
    rows = side_ref.shape[2]
    core = place_ref[1]
    even = core == 0
    scale = 1.0 / dim**0.5
    lead = 3 * rows
    chunk = 256

    def soft(h):
        for s, win in ((0, kw_ref.at[h]), (1, vw_buf.at[h])):
            win[:rows, :] = jnp.where(even, side_ref[s, h], both_ref[1 - core, s, h])
            win[rows : 2 * rows, :] = both_ref[core, s, h]
            win[2 * rows :, :] = jnp.where(even, both_ref[1 - core, s, h], side_ref[s, h])
        for c in range(n_rows // chunk):
            cols = slice(c * chunk, (c + 1) * chunk)
            s = lax.dot_general(kw_ref[h], qs_ref[h, cols, :], NT, preferred_element_type=F32)
            dp = lax.dot_general(vw_buf[h], gs_ref[h, cols, :], NT, preferred_element_type=F32)
            kp = lax.broadcasted_iota(jnp.int32, (lead, chunk), 0)
            s = jnp.where(kp >= low_ref[0:1, cols], s, -1e30)
            old = stat_ref[h, 0:1, cols]
            top = jnp.maximum(jnp.max(s, axis=0, keepdims=True), old)
            e = jnp.exp2((s - top) * (scale * LOG2E))
            keep = jnp.exp2((old - top) * (scale * LOG2E))
            r = 1.0 / (jnp.sum(e, axis=0, keepdims=True) + keep * stat_ref[h, 1:2, cols])
            delta = (jnp.sum(e * dp, axis=0, keepdims=True) + keep * stat_ref[h, 2:3, cols]) * r
            final_ref[h, 0:1, cols] = top
            final_ref[h, 1:2, cols] = r
            final_ref[h, 2:3, cols] = delta
            p = e * r
            ps_buf[h, :, cols] = p.astype(BF)
            ds_ref[h, :, cols] = (p * (dp - delta)).astype(BF)

    def sums(h):
        dk = (jnp.dot(ds_ref[h], qs_ref[h], preferred_element_type=F32) * scale).astype(BF)
        dv = jnp.dot(ps_buf[h], gs_ref[h], preferred_element_type=F32).astype(BF)
        for s, x in ((0, dk), (1, dv)):
            base_ref[s, h] = x[rows : 2 * rows]
            away_ref[s, h] = jnp.where(even, x[:rows], x[2 * rows :])
            cross_ref[s, h] = jnp.where(even, x[2 * rows :], x[:rows])

    for h in range(kv_heads):
        soft(h)
        if h:
            sums(h - 1)
    sums(kv_heads - 1)


def own_part(low_ref, final_ref, qs_ref, gs_ref, own_ref, dso_ref, loc_ref):
    kv_heads, n_rows, dim = qs_ref.shape
    rows = own_ref.shape[2]
    scale = 1.0 / dim**0.5
    allowed = diagonal(low_ref[0:1, :], rows, n_rows)
    for h in range(kv_heads):
        s = lax.dot_general(own_ref[0, h], qs_ref[h], NT, preferred_element_type=F32)
        dp = lax.dot_general(own_ref[1, h], gs_ref[h], NT, preferred_element_type=F32)
        s = jnp.where(allowed, s, -1e30)
        p = jnp.exp2((s - final_ref[h, 0:1, :]) * (scale * LOG2E)) * final_ref[h, 1:2, :]
        ds = (p * (dp - final_ref[h, 2:3, :])).astype(BF)
        dso_ref[h] = ds
        loc_ref[0, h] = jnp.dot(ds, qs_ref[h], preferred_element_type=F32) * scale
        loc_ref[1, h] = jnp.dot(p.astype(BF), gs_ref[h], preferred_element_type=F32)


def query_part(ds_ref, kw_ref, dso_ref, own_ref, dq_ref, dq_all, out_buf, sems):
    kv_heads, _, n_rows = ds_ref.shape
    rows, dim = own_ref.shape[2:]
    group = n_rows // rows
    heads = kv_heads * group
    step = 256 // heads
    scale = 1.0 / dim**0.5
    for h in range(kv_heads):
        dq = lax.dot_general(kw_ref[h], ds_ref[h], TN, preferred_element_type=F32)
        dq = (dq + lax.dot_general(own_ref[0, h], dso_ref[h], TN, preferred_element_type=F32)) * scale
        for x in range(group):
            dq_all[h * group + x] = dq[:, x * rows : (x + 1) * rows].T.astype(BF)
    turn = to_tokens(heads)
    copies = []
    half = rows * heads // 2
    for ch in range(rows // step):
        block = dq_all[:, ch * step : (ch + 1) * step, :].reshape(256, dim)
        out_buf[ch * 256 : (ch + 1) * 256, :] = pick(turn, block)
        if (ch + 1) * 256 % half == 0:
            at = pl.ds(len(copies) * half, half)
            copies.append(pltpu.make_async_copy(out_buf.at[at, :], dq_ref.at[at, :], sems.at[len(copies)]))
            copies[-1].start()
    for copy in copies:
        copy.wait()


def finish(loc_ref, back_ref, away_ref, dk_ref, dv_ref, buf, sems):
    _, kv_heads, rows, dim = loc_ref.shape
    tok = 256 // kv_heads
    turn = to_tokens(kv_heads)
    copies = []
    for s, out in ((0, dk_ref), (1, dv_ref)):
        for ch in range(rows // tok):
            at = (s, slice(None), slice(ch * tok, (ch + 1) * tok), slice(None))
            total = loc_ref[at] + away_ref[at].astype(F32)
            total = total + back_ref[at].astype(F32)
            buf[s, ch * 256 : (ch + 1) * 256, :] = pick(turn, total.astype(BF).reshape(256, dim))
        copies.append(pltpu.make_async_copy(buf.at[s], out, sems.at[s]))
        copies[-1].start()
    for copy in copies:
        copy.wait()


def body(queries, keys, values, out_grad, lengths):
    rows, heads, dim = queries.shape
    kv_heads = keys.shape[1]
    n_rows = heads // kv_heads * rows
    lead = 3 * rows
    n = lax.axis_size("dp") * lax.axis_size("ctx")
    core = lax.rem(lax.axis_index("ctx"), 2)
    place = jnp.stack([lax.axis_index(AXES) * rows, core]).astype(jnp.int32)
    shape = jax.ShapeDtypeStruct
    sums = (2, kv_heads, rows, dim)

    def mixed(even, odd):
        steps = [(i, i + (odd if i % 2 else even)) for i in range(n)]
        return [(i, j) for i, j in steps if 0 <= j < n]

    hbm = lambda x: pltpu.with_memory_space_constraint(x, pltpu.HBM)
    own = pl.pallas_call(
        pack,
        in_specs=[IN_HBM] * 2,
        out_shape=shape(sums, BF),
        out_specs=IN_VMEM,
        scratch_shapes=[pltpu.VMEM((rows * kv_heads, dim), BF)] * 2 + [pltpu.SemaphoreType.DMA((2,))],
        compiler_params=PARAMS,
        name="pack",
    )(hbm(keys.reshape(rows * kv_heads, dim)), hbm(values.reshape(rows * kv_heads, dim)))

    got = lax.ppermute(own, AXES, mixed(2, 2))
    side = lax.ppermute(own, AXES, mixed(1, 3))
    qs, gs, low, stat = pl.pallas_call(
        prepare,
        in_specs=[IN_SMEM, IN_VMEM, IN_HBM, IN_HBM, IN_VMEM],
        out_shape=[shape((kv_heads, n_rows, dim), BF)] * 2 + [shape((8, n_rows), jnp.int32), shape((kv_heads, 8, n_rows), F32)],
        out_specs=[IN_VMEM] * 4,
        scratch_shapes=[pltpu.VMEM((rows * heads, dim), BF)] * 2 + [pltpu.SemaphoreType.DMA((2,))],
        compiler_params=PARAMS,
        cost_estimate=pl.CostEstimate(flops=1_000_000_000, bytes_accessed=4_000_000, transcendentals=1 << 18),
        name="prepare",
    )(place, lengths.reshape(1, -1), hbm(queries.reshape(rows * heads, dim)), hbm(out_grad.reshape(rows * heads, dim)), own)
    got, qs = lax.optimization_barrier((got, qs))
    pairs = [[2 * i, 2 * i + 1] for i in range(lax.axis_size("ctx") // 2)]
    both = lax.all_gather(got, "ctx", axis_index_groups=pairs)

    ds, kw, final, away, cross, base = pl.pallas_call(
        attend,
        in_specs=[IN_SMEM] + [IN_VMEM] * 6,
        out_shape=[shape((kv_heads, lead, n_rows), BF), shape((kv_heads, lead, dim), BF), shape((kv_heads, 8, n_rows), F32)]
        + [shape(sums, BF)] * 3,
        out_specs=[IN_VMEM] * 6,
        scratch_shapes=[pltpu.VMEM((kv_heads, lead, n_rows), BF), pltpu.VMEM((kv_heads, lead, dim), BF)],
        compiler_params=PARAMS,
        cost_estimate=pl.CostEstimate(flops=1_000_000_000, bytes_accessed=8_000_000, transcendentals=1 << 20),
        name="attend",
    )(place, low, stat, qs, gs, side, both)

    away_got = lax.ppermute(away, AXES, mixed(-3, -1))
    crossed = lax.all_gather(cross, "ctx", axis_index_groups=pairs)
    crossed = lax.dynamic_index_in_dim(crossed, 1 - core, 0, keepdims=False)
    part = (base.astype(F32) + crossed.astype(F32)).astype(BF)
    back = lax.ppermute(part, AXES, mixed(-2, -2))
    part, final, kw = lax.optimization_barrier((part, final, kw))
    dso, loc = pl.pallas_call(
        own_part,
        in_specs=[IN_VMEM] * 5,
        out_shape=[shape((kv_heads, rows, n_rows), BF), shape(sums, F32)],
        out_specs=[IN_VMEM] * 2,
        compiler_params=PARAMS,
        cost_estimate=pl.CostEstimate(flops=300_000_000, bytes_accessed=4_000_000, transcendentals=1 << 18),
        name="own_part",
    )(low, final, qs, gs, own)
    dq = pl.pallas_call(
        query_part,
        in_specs=[IN_VMEM] * 4,
        out_shape=shape((rows * heads, dim), BF),
        out_specs=IN_HBM,
        scratch_shapes=[pltpu.VMEM((heads, rows, dim), BF), pltpu.VMEM((rows * heads, dim), BF), pltpu.SemaphoreType.DMA((2,))],
        compiler_params=PARAMS,
        cost_estimate=pl.CostEstimate(flops=800_000_000, bytes_accessed=4_000_000, transcendentals=0),
        name="query_part",
    )(ds, kw, dso, own)

    dk, dv = pl.pallas_call(
        finish,
        in_specs=[IN_VMEM] * 3,
        out_shape=[shape((rows * kv_heads, dim), BF)] * 2,
        out_specs=[IN_HBM] * 2,
        scratch_shapes=[pltpu.VMEM((2, rows * kv_heads, dim), BF), pltpu.SemaphoreType.DMA((2,))],
        compiler_params=PARAMS,
        name="finish",
    )(loc, back, away_got)
    return dq.reshape(rows, heads, dim), dk.reshape(rows, kv_heads, dim), dv.reshape(rows, kv_heads, dim)


def solution(mesh):
    token = P(AXES, None, None)
    return jax.shard_map(
        body,
        mesh=mesh,
        in_specs=(token, token, token, token, P()),
        out_specs=(token, token, token),
        check_vma=False,
    )
```

```python
import jax
import jax.numpy as jnp
from jax import lax
from jax.experimental import pallas as pl
from jax.experimental.pallas import tpu as pltpu
from jax.sharding import PartitionSpec as P

AXES = ("dp", "ctx")
BF = jnp.bfloat16
F32 = jnp.float32
VMEM = 28 * 1024 * 1024
NT = (((1,), (1,)), ((), ()))
TN = (((0,), (0,)), ((), ()))
LOG2E = 1.4426950408889634
PARAMS = pltpu.CompilerParams(vmem_limit_bytes=VMEM)
IN_SMEM = pl.BlockSpec(memory_space=pltpu.SMEM)
IN_VMEM = pl.BlockSpec(memory_space=pltpu.VMEM)
IN_HBM = pl.BlockSpec(memory_space=pltpu.HBM)


def hot(source):
    o = lax.broadcasted_iota(jnp.int32, (256, 256), 0)
    r = lax.broadcasted_iota(jnp.int32, (256, 256), 1)
    return jnp.where(r == source(o), 1.0, 0.0).astype(BF)


def pick(onehot, block):
    return jnp.dot(onehot, block, preferred_element_type=F32).astype(BF)


def to_heads(heads):
    step = 256 // heads
    return hot(lambda o: lax.rem(o, step) * heads + o // step)


def to_tokens(heads):
    step = 256 // heads
    return hot(lambda o: lax.rem(o, heads) * step + o // heads)


def pack(k_ref, v_ref, own_ref, k_buf, v_buf, sems):
    copies = [pltpu.make_async_copy(src, dst, sems.at[i]) for i, (src, dst) in enumerate(((k_ref, k_buf), (v_ref, v_buf)))]
    for copy in copies:
        copy.start()
    _, heads, rows, _ = own_ref.shape
    step = 256 // heads
    turn = to_heads(heads)
    for s, buf in enumerate((k_buf, v_buf)):
        copies[s].wait()
        for ch in range(rows // step):
            got = pick(turn, buf[ch * 256 : (ch + 1) * 256, :])
            for h in range(heads):
                own_ref[s, h, ch * step : (ch + 1) * step, :] = got[h * step : (h + 1) * step, :]


def diagonal(low, rows, n_rows):
    kp = lax.broadcasted_iota(jnp.int32, (rows, n_rows), 0)
    tq = lax.rem(lax.broadcasted_iota(jnp.int32, (1, n_rows), 1), rows)
    return (kp + 3 * rows >= low) & (kp <= tq)


def prepare(place_ref, len_ref, q_ref, g_ref, own_ref, qs_ref, gs_ref, low_ref, stat_ref, q_buf, g_buf, sems):
    copies = [pltpu.make_async_copy(src, dst, sems.at[i]) for i, (src, dst) in enumerate(((q_ref, q_buf), (g_ref, g_buf)))]
    for copy in copies:
        copy.start()
    kv_heads, n_rows, dim = qs_ref.shape
    rows = own_ref.shape[2]
    group = n_rows // rows
    heads = kv_heads * group
    n_docs = len_ref.shape[1]
    step = 256 // heads
    turn = to_heads(heads)
    start = place_ref[0]
    i = lax.broadcasted_iota(jnp.int32, (n_docs, n_docs), 1)
    j = lax.broadcasted_iota(jnp.int32, (n_docs, n_docs), 0)
    ends = jnp.sum(jnp.where(i <= j, len_ref[...], 0), axis=1, keepdims=True)
    pos = start + lax.rem(lax.broadcasted_iota(jnp.int32, (1, n_rows), 1), rows)
    first = jnp.max(jnp.where(ends <= pos, ends, 0), axis=0, keepdims=True)
    low = first - (start - 3 * rows)
    low_ref[...] = jnp.broadcast_to(low, low_ref.shape)
    for s, (buf, dst) in enumerate(((q_buf, qs_ref), (g_buf, gs_ref))):
        copies[s].wait()
        for ch in range(rows // step):
            got = pick(turn, buf[ch * 256 : (ch + 1) * 256, :])
            for h in range(heads):
                at = (h % group) * rows + ch * step
                dst[h // group, at : at + step, :] = got[h * step : (h + 1) * step, :]
    allowed = diagonal(low, rows, n_rows)
    for h in range(kv_heads):
        s = lax.dot_general(own_ref[0, h], qs_ref[h], NT, preferred_element_type=F32)
        dp = lax.dot_general(own_ref[1, h], gs_ref[h], NT, preferred_element_type=F32)
        s = jnp.where(allowed, s, -1e30)
        top = jnp.max(s, axis=0, keepdims=True)
        e = jnp.exp2((s - top) * (LOG2E / dim**0.5))
        stat_ref[h, 0:1, :] = top
        stat_ref[h, 1:2, :] = jnp.sum(e, axis=0, keepdims=True)
        stat_ref[h, 2:3, :] = jnp.sum(e * dp, axis=0, keepdims=True)


def attend_two(low_ref, stat_ref, qs_ref, gs_ref, both_ref, kw_ref, e_ref, dp_ref, next_ref, vw_buf):
    kv_heads, n_rows, dim = qs_ref.shape
    rows = kw_ref.shape[1] // 2
    core = lax.rem(lax.axis_index(AXES), 2)
    chunk = 256
    for h in range(kv_heads):
        kw_ref[h, :rows, :] = both_ref[core, 0, h]
        kw_ref[h, rows:, :] = both_ref[1 - core, 0, h]
        vw_buf[h, :rows, :] = both_ref[core, 1, h]
        vw_buf[h, rows:, :] = both_ref[1 - core, 1, h]
    kp = lax.broadcasted_iota(jnp.int32, (2 * rows, chunk), 0)
    kp = jnp.where(kp < rows, kp + rows, kp - rows + 2 * rows * (1 - core))
    for h in range(kv_heads):
        for c in range(n_rows // chunk):
            cols = slice(c * chunk, (c + 1) * chunk)
            s = lax.dot_general(kw_ref[h], qs_ref[h, cols, :], NT, preferred_element_type=F32)
            dp = lax.dot_general(vw_buf[h], gs_ref[h, cols, :], NT, preferred_element_type=F32)
            s = jnp.where(kp >= low_ref[0:1, cols], s, -1e30)
            old = stat_ref[h, 0:1, cols]
            top = jnp.maximum(jnp.max(s, axis=0, keepdims=True), old)
            e = jnp.exp2((s - top) * (LOG2E / dim**0.5))
            keep = jnp.exp2((old - top) * (LOG2E / dim**0.5))
            e_ref[h, :, cols] = e
            dp_ref[h, :, cols] = dp
            next_ref[h, 0:1, cols] = top
            next_ref[h, 1:2, cols] = jnp.sum(e, axis=0, keepdims=True) + keep * stat_ref[h, 1:2, cols]
            next_ref[h, 2:3, cols] = jnp.sum(e * dp, axis=0, keepdims=True) + keep * stat_ref[h, 2:3, cols]


def attend(low_ref, stat_ref, qs_ref, gs_ref, e_ref, dp_ref, side_ref,
           ds_ref, final_ref, away_ref, cross_ref, base_ref, ps_buf):
    kv_heads, n_rows, dim = qs_ref.shape
    rows = side_ref.shape[2]
    two = 2 * rows
    scale = 1.0 / dim**0.5
    chunk = 256
    kp = lax.broadcasted_iota(jnp.int32, (rows, chunk), 0) + two * lax.rem(lax.axis_index(AXES), 2)

    def soft(h):
        for c in range(n_rows // chunk):
            cols = slice(c * chunk, (c + 1) * chunk)
            s = lax.dot_general(side_ref[0, h], qs_ref[h, cols, :], NT, preferred_element_type=F32)
            dp = lax.dot_general(side_ref[1, h], gs_ref[h, cols, :], NT, preferred_element_type=F32)
            s = jnp.where(kp >= low_ref[0:1, cols], s, -1e30)
            old = stat_ref[h, 0:1, cols]
            top = jnp.maximum(jnp.max(s, axis=0, keepdims=True), old)
            e = jnp.exp2((s - top) * (scale * LOG2E))
            keep = jnp.exp2((old - top) * (scale * LOG2E))
            r = 1.0 / (jnp.sum(e, axis=0, keepdims=True) + keep * stat_ref[h, 1:2, cols])
            delta = (jnp.sum(e * dp, axis=0, keepdims=True) + keep * stat_ref[h, 2:3, cols]) * r
            final_ref[h, 0:1, cols] = top
            final_ref[h, 1:2, cols] = r
            final_ref[h, 2:3, cols] = delta
            p = e * r
            ps_buf[h, two:, cols] = p.astype(BF)
            ds_ref[h, two:, cols] = (p * (dp - delta)).astype(BF)
            p = e_ref[h, :, cols] * (keep * r)
            ps_buf[h, :two, cols] = p.astype(BF)
            ds_ref[h, :two, cols] = (p * (dp_ref[h, :, cols] - delta)).astype(BF)

    def sums(h):
        dk = (jnp.dot(ds_ref[h], qs_ref[h], preferred_element_type=F32) * scale).astype(BF)
        dv = jnp.dot(ps_buf[h], gs_ref[h], preferred_element_type=F32).astype(BF)
        for s, x in ((0, dk), (1, dv)):
            base_ref[s, h] = x[:rows]
            cross_ref[s, h] = x[rows:two]
            away_ref[s, h] = x[two:]

    for h in range(kv_heads):
        soft(h)
        if h:
            sums(h - 1)
    sums(kv_heads - 1)


def own_part(low_ref, final_ref, qs_ref, gs_ref, own_ref, dso_ref, loc_ref):
    kv_heads, n_rows, dim = qs_ref.shape
    rows = own_ref.shape[2]
    scale = 1.0 / dim**0.5
    allowed = diagonal(low_ref[0:1, :], rows, n_rows)
    for h in range(kv_heads):
        s = lax.dot_general(own_ref[0, h], qs_ref[h], NT, preferred_element_type=F32)
        dp = lax.dot_general(own_ref[1, h], gs_ref[h], NT, preferred_element_type=F32)
        s = jnp.where(allowed, s, -1e30)
        p = jnp.exp2((s - final_ref[h, 0:1, :]) * (scale * LOG2E)) * final_ref[h, 1:2, :]
        ds = (p * (dp - final_ref[h, 2:3, :])).astype(BF)
        dso_ref[h] = ds
        loc_ref[0, h] = jnp.dot(ds, qs_ref[h], preferred_element_type=F32) * scale
        loc_ref[1, h] = jnp.dot(p.astype(BF), gs_ref[h], preferred_element_type=F32)


def query_part(ds_ref, kw_ref, side_ref, dso_ref, own_ref, dq_ref, dq_all, out_buf, sems):
    kv_heads, _, n_rows = ds_ref.shape
    rows, dim = own_ref.shape[2:]
    group = n_rows // rows
    heads = kv_heads * group
    step = 256 // heads
    scale = 1.0 / dim**0.5
    for h in range(kv_heads):
        dq = lax.dot_general(kw_ref[h], ds_ref[h, : 2 * rows, :], TN, preferred_element_type=F32)
        dq = dq + lax.dot_general(side_ref[0, h], ds_ref[h, 2 * rows :, :], TN, preferred_element_type=F32)
        dq = (dq + lax.dot_general(own_ref[0, h], dso_ref[h], TN, preferred_element_type=F32)) * scale
        for x in range(group):
            dq_all[h * group + x] = dq[:, x * rows : (x + 1) * rows].T.astype(BF)
    turn = to_tokens(heads)
    copies = []
    half = rows * heads // 2
    for ch in range(rows // step):
        block = dq_all[:, ch * step : (ch + 1) * step, :].reshape(256, dim)
        out_buf[ch * 256 : (ch + 1) * 256, :] = pick(turn, block)
        if (ch + 1) * 256 % half == 0:
            at = pl.ds(len(copies) * half, half)
            copies.append(pltpu.make_async_copy(out_buf.at[at, :], dq_ref.at[at, :], sems.at[len(copies)]))
            copies[-1].start()
    for copy in copies:
        copy.wait()


def finish(loc_ref, back_ref, away_ref, dk_ref, dv_ref, buf, sems):
    _, kv_heads, rows, dim = loc_ref.shape
    tok = 256 // kv_heads
    turn = to_tokens(kv_heads)
    copies = []
    for s, out in ((0, dk_ref), (1, dv_ref)):
        for ch in range(rows // tok):
            at = (s, slice(None), slice(ch * tok, (ch + 1) * tok), slice(None))
            total = loc_ref[at] + away_ref[at].astype(F32)
            total = total + back_ref[at].astype(F32)
            buf[s, ch * 256 : (ch + 1) * 256, :] = pick(turn, total.astype(BF).reshape(256, dim))
        copies.append(pltpu.make_async_copy(buf.at[s], out, sems.at[s]))
        copies[-1].start()
    for copy in copies:
        copy.wait()


def body(queries, keys, values, out_grad, lengths):
    rows, heads, dim = queries.shape
    kv_heads = keys.shape[1]
    n_rows = heads // kv_heads * rows
    lead = 3 * rows
    n = lax.axis_size("dp") * lax.axis_size("ctx")
    core = lax.rem(lax.axis_index("ctx"), 2)
    place = jnp.stack([lax.axis_index(AXES) * rows]).astype(jnp.int32)
    shape = jax.ShapeDtypeStruct
    sums = (2, kv_heads, rows, dim)

    def mixed(even, odd):
        steps = [(i, i + (odd if i % 2 else even)) for i in range(n)]
        return [(i, j) for i, j in steps if 0 <= j < n]

    hbm = lambda x: pltpu.with_memory_space_constraint(x, pltpu.HBM)
    k_flat, v_flat = keys.reshape(rows * kv_heads, dim), values.reshape(rows * kv_heads, dim)

    own = pl.pallas_call(
        pack,
        in_specs=[IN_HBM] * 2,
        out_shape=shape(sums, BF),
        out_specs=IN_VMEM,
        scratch_shapes=[pltpu.VMEM((rows * kv_heads, dim), BF)] * 2 + [pltpu.SemaphoreType.DMA((2,))],
        compiler_params=PARAMS,
        name="pack",
    )(hbm(k_flat), hbm(v_flat))

    got = lax.ppermute(own, AXES, mixed(2, 2))
    side = lax.ppermute(own, AXES, mixed(1, 3))
    qs, gs, low, stat = pl.pallas_call(
        prepare,
        in_specs=[IN_SMEM, IN_VMEM, IN_HBM, IN_HBM, IN_VMEM],
        out_shape=[shape((kv_heads, n_rows, dim), BF)] * 2 + [shape((8, n_rows), jnp.int32), shape((kv_heads, 8, n_rows), F32)],
        out_specs=[IN_VMEM] * 4,
        scratch_shapes=[pltpu.VMEM((rows * heads, dim), BF)] * 2 + [pltpu.SemaphoreType.DMA((2,))],
        compiler_params=PARAMS,
        cost_estimate=pl.CostEstimate(flops=1_000_000_000, bytes_accessed=4_000_000, transcendentals=1 << 18),
        name="prepare",
    )(place, lengths.reshape(1, -1), hbm(queries.reshape(rows * heads, dim)), hbm(out_grad.reshape(rows * heads, dim)), own)
    got, qs = lax.optimization_barrier((got, qs))
    pairs = [[2 * i, 2 * i + 1] for i in range(lax.axis_size("ctx") // 2)]
    both = lax.all_gather(got, "ctx", axis_index_groups=pairs)

    kw_ab, e_ab, dp_ab, stat = pl.pallas_call(
        attend_two,
        in_specs=[IN_VMEM] * 5,
        out_shape=[shape((kv_heads, 2 * rows, dim), BF), shape((kv_heads, 2 * rows, n_rows), F32)]
        + [shape((kv_heads, 2 * rows, n_rows), F32), shape((kv_heads, 8, n_rows), F32)],
        out_specs=[IN_VMEM] * 4,
        scratch_shapes=[pltpu.VMEM((kv_heads, 2 * rows, dim), BF)],
        compiler_params=PARAMS,
        name="attend_two",
    )(low, stat, qs, gs, both)
    ds, final, away, cross, base = pl.pallas_call(
        attend,
        in_specs=[IN_VMEM] * 7,
        out_shape=[shape((kv_heads, lead, n_rows), BF), shape((kv_heads, 8, n_rows), F32)] + [shape(sums, BF)] * 3,
        out_specs=[IN_VMEM] * 5,
        scratch_shapes=[pltpu.VMEM((kv_heads, lead, n_rows), BF)],
        compiler_params=PARAMS,
        name="attend",
    )(low, stat, qs, gs, e_ab, dp_ab, side)

    away_got = lax.ppermute(away, AXES, mixed(-3, -1))
    crossed = lax.all_gather(cross, "ctx", axis_index_groups=pairs)
    crossed = lax.dynamic_index_in_dim(crossed, 1 - core, 0, keepdims=False)
    part = (base.astype(F32) + crossed.astype(F32)).astype(BF)
    back = lax.ppermute(part, AXES, mixed(-2, -2))
    part, final, kw_ab = lax.optimization_barrier((part, final, kw_ab))
    dso, loc = pl.pallas_call(
        own_part,
        in_specs=[IN_VMEM] * 5,
        out_shape=[shape((kv_heads, rows, n_rows), BF), shape(sums, F32)],
        out_specs=[IN_VMEM] * 2,
        compiler_params=PARAMS,
        cost_estimate=pl.CostEstimate(flops=300_000_000, bytes_accessed=4_000_000, transcendentals=1 << 18),
        name="own_part",
    )(low, final, qs, gs, own)
    dq = pl.pallas_call(
        query_part,
        in_specs=[IN_VMEM] * 5,
        out_shape=shape((rows * heads, dim), BF),
        out_specs=IN_HBM,
        scratch_shapes=[pltpu.VMEM((heads, rows, dim), BF), pltpu.VMEM((rows * heads, dim), BF), pltpu.SemaphoreType.DMA((2,))],
        compiler_params=PARAMS,
        cost_estimate=pl.CostEstimate(flops=800_000_000, bytes_accessed=4_000_000, transcendentals=0),
        name="query_part",
    )(ds, kw_ab, side, dso, own)

    dk, dv = pl.pallas_call(
        finish,
        in_specs=[IN_VMEM] * 3,
        out_shape=[shape((rows * kv_heads, dim), BF)] * 2,
        out_specs=[IN_HBM] * 2,
        scratch_shapes=[pltpu.VMEM((2, rows * kv_heads, dim), BF), pltpu.SemaphoreType.DMA((2,))],
        compiler_params=PARAMS,
        name="finish",
    )(loc, back, away_got)
    return dq.reshape(rows, heads, dim), dk.reshape(rows, kv_heads, dim), dv.reshape(rows, kv_heads, dim)


def solution(mesh):
    token = P(AXES, None, None)
    return jax.shard_map(
        body,
        mesh=mesh,
        in_specs=(token, token, token, token, P()),
        out_specs=(token, token, token),
        check_vma=False,
    )
```

```python
import jax
import jax.numpy as jnp
from jax import lax
from jax.experimental import pallas as pl
from jax.experimental.pallas import tpu as pltpu
from jax.sharding import PartitionSpec as P

AXES = ("dp", "ctx")
BF = jnp.bfloat16
F32 = jnp.float32
VMEM = 28 * 1024 * 1024
NT = (((1,), (1,)), ((), ()))
TN = (((0,), (0,)), ((), ()))
LOG2E = 1.4426950408889634
PARAMS = pltpu.CompilerParams(vmem_limit_bytes=VMEM)
IN_SMEM = pl.BlockSpec(memory_space=pltpu.SMEM)
IN_VMEM = pl.BlockSpec(memory_space=pltpu.VMEM)
IN_HBM = pl.BlockSpec(memory_space=pltpu.HBM)


def hot(source):
    o = lax.broadcasted_iota(jnp.int32, (256, 256), 0)
    r = lax.broadcasted_iota(jnp.int32, (256, 256), 1)
    return jnp.where(r == source(o), 1.0, 0.0).astype(BF)


def pick(onehot, block):
    return jnp.dot(onehot, block, preferred_element_type=F32).astype(BF)


def to_heads(heads):
    step = 256 // heads
    return hot(lambda o: lax.rem(o, step) * heads + o // step)


def to_tokens(heads):
    step = 256 // heads
    return hot(lambda o: lax.rem(o, heads) * step + o // heads)


def pack(k_ref, v_ref, own_ref, k_buf, v_buf, sems):
    copies = [pltpu.make_async_copy(src, dst, sems.at[i]) for i, (src, dst) in enumerate(((k_ref, k_buf), (v_ref, v_buf)))]
    for copy in copies:
        copy.start()
    _, heads, rows, _ = own_ref.shape
    step = 256 // heads
    turn = to_heads(heads)
    for s, buf in enumerate((k_buf, v_buf)):
        copies[s].wait()
        for ch in range(rows // step):
            got = pick(turn, buf[ch * 256 : (ch + 1) * 256, :])
            for h in range(heads):
                own_ref[s, h, ch * step : (ch + 1) * step, :] = got[h * step : (h + 1) * step, :]


def diagonal(low, rows, n_rows):
    kp = lax.broadcasted_iota(jnp.int32, (rows, n_rows), 0)
    tq = lax.rem(lax.broadcasted_iota(jnp.int32, (1, n_rows), 1), rows)
    return (kp + 3 * rows >= low) & (kp <= tq)


def prepare(place_ref, len_ref, q_ref, g_ref, own_ref, qs_ref, gs_ref, low_ref, stat_ref, q_buf, g_buf, sems):
    copies = [pltpu.make_async_copy(src, dst, sems.at[i]) for i, (src, dst) in enumerate(((q_ref, q_buf), (g_ref, g_buf)))]
    for copy in copies:
        copy.start()
    kv_heads, n_rows, dim = qs_ref.shape
    rows = own_ref.shape[2]
    group = n_rows // rows
    heads = kv_heads * group
    n_docs = len_ref.shape[1]
    step = 256 // heads
    turn = to_heads(heads)
    start = place_ref[0]
    i = lax.broadcasted_iota(jnp.int32, (n_docs, n_docs), 1)
    j = lax.broadcasted_iota(jnp.int32, (n_docs, n_docs), 0)
    ends = jnp.sum(jnp.where(i <= j, len_ref[...], 0), axis=1, keepdims=True)
    pos = start + lax.rem(lax.broadcasted_iota(jnp.int32, (1, n_rows), 1), rows)
    first = jnp.max(jnp.where(ends <= pos, ends, 0), axis=0, keepdims=True)
    low = first - (start - 3 * rows)
    low_ref[...] = jnp.broadcast_to(low, low_ref.shape)
    for s, (buf, dst) in enumerate(((q_buf, qs_ref), (g_buf, gs_ref))):
        copies[s].wait()
        for ch in range(rows // step):
            got = pick(turn, buf[ch * 256 : (ch + 1) * 256, :])
            for h in range(heads):
                at = (h % group) * rows + ch * step
                dst[h // group, at : at + step, :] = got[h * step : (h + 1) * step, :]
    allowed = diagonal(low, rows, n_rows)
    for h in range(kv_heads):
        s = lax.dot_general(own_ref[0, h], qs_ref[h], NT, preferred_element_type=F32)
        dp = lax.dot_general(own_ref[1, h], gs_ref[h], NT, preferred_element_type=F32)
        s = jnp.where(allowed, s, -1e30)
        top = jnp.max(s, axis=0, keepdims=True)
        e = jnp.exp2((s - top) * (LOG2E / dim**0.5))
        stat_ref[h, 0:1, :] = top
        stat_ref[h, 1:2, :] = jnp.sum(e, axis=0, keepdims=True)
        stat_ref[h, 2:3, :] = jnp.sum(e * dp, axis=0, keepdims=True)


def attend_two(low_ref, stat_ref, qs_ref, gs_ref, both_ref, kw_ref, e_ref, dp_ref, next_ref, vw_buf):
    kv_heads, n_rows, dim = qs_ref.shape
    rows = kw_ref.shape[1] // 2
    core = lax.rem(lax.axis_index(AXES), 2)
    chunk = 256
    for h in range(kv_heads):
        kw_ref[h, :rows, :] = both_ref[core, 0, h]
        kw_ref[h, rows:, :] = both_ref[1 - core, 0, h]
        vw_buf[h, :rows, :] = both_ref[core, 1, h]
        vw_buf[h, rows:, :] = both_ref[1 - core, 1, h]
    kp = lax.broadcasted_iota(jnp.int32, (2 * rows, chunk), 0)
    kp = jnp.where(kp < rows, kp + rows, kp - rows + 2 * rows * (1 - core))
    for h in range(kv_heads):
        for c in range(n_rows // chunk):
            cols = slice(c * chunk, (c + 1) * chunk)
            s = lax.dot_general(kw_ref[h], qs_ref[h, cols, :], NT, preferred_element_type=F32)
            dp = lax.dot_general(vw_buf[h], gs_ref[h, cols, :], NT, preferred_element_type=F32)
            s = jnp.where(kp >= low_ref[0:1, cols], s, -1e30)
            old = stat_ref[h, 0:1, cols]
            top = jnp.maximum(jnp.max(s, axis=0, keepdims=True), old)
            e = jnp.exp2((s - top) * (LOG2E / dim**0.5))
            keep = jnp.exp2((old - top) * (LOG2E / dim**0.5))
            e_ref[h, :, cols] = e
            dp_ref[h, :, cols] = dp
            next_ref[h, 0:1, cols] = top
            next_ref[h, 1:2, cols] = jnp.sum(e, axis=0, keepdims=True) + keep * stat_ref[h, 1:2, cols]
            next_ref[h, 2:3, cols] = jnp.sum(e * dp, axis=0, keepdims=True) + keep * stat_ref[h, 2:3, cols]


def attend(low_ref, stat_ref, qs_ref, gs_ref, e_ref, dp_ref, straight_ref, relayed_ref,
           ds_ref, final_ref, away_ref, cross_ref, base_ref, ps_buf):
    kv_heads, n_rows, dim = qs_ref.shape
    rows = straight_ref.shape[2]
    two = 2 * rows
    scale = 1.0 / dim**0.5
    chunk = 256
    kp = lax.broadcasted_iota(jnp.int32, (rows, chunk), 0) + two * lax.rem(lax.axis_index(AXES), 2)

    def soft(h):
        keys, vals = straight_ref[0, h] + relayed_ref[0, h], straight_ref[1, h] + relayed_ref[1, h]
        for c in range(n_rows // chunk):
            cols = slice(c * chunk, (c + 1) * chunk)
            s = lax.dot_general(keys, qs_ref[h, cols, :], NT, preferred_element_type=F32)
            dp = lax.dot_general(vals, gs_ref[h, cols, :], NT, preferred_element_type=F32)
            s = jnp.where(kp >= low_ref[0:1, cols], s, -1e30)
            old = stat_ref[h, 0:1, cols]
            top = jnp.maximum(jnp.max(s, axis=0, keepdims=True), old)
            e = jnp.exp2((s - top) * (scale * LOG2E))
            keep = jnp.exp2((old - top) * (scale * LOG2E))
            r = 1.0 / (jnp.sum(e, axis=0, keepdims=True) + keep * stat_ref[h, 1:2, cols])
            delta = (jnp.sum(e * dp, axis=0, keepdims=True) + keep * stat_ref[h, 2:3, cols]) * r
            final_ref[h, 0:1, cols] = top
            final_ref[h, 1:2, cols] = r
            final_ref[h, 2:3, cols] = delta
            p = e * r
            ps_buf[h, two:, cols] = p.astype(BF)
            ds_ref[h, two:, cols] = (p * (dp - delta)).astype(BF)
            p = e_ref[h, :, cols] * (keep * r)
            ps_buf[h, :two, cols] = p.astype(BF)
            ds_ref[h, :two, cols] = (p * (dp_ref[h, :, cols] - delta)).astype(BF)

    def sums(h):
        dk = (jnp.dot(ds_ref[h], qs_ref[h], preferred_element_type=F32) * scale).astype(BF)
        dv = jnp.dot(ps_buf[h], gs_ref[h], preferred_element_type=F32).astype(BF)
        for s, x in ((0, dk), (1, dv)):
            base_ref[s, h] = x[:rows]
            cross_ref[s, h] = x[rows:two]
            away_ref[s, h] = x[two:]

    for h in range(kv_heads):
        soft(h)
        if h:
            sums(h - 1)
    sums(kv_heads - 1)


def own_part(low_ref, final_ref, qs_ref, gs_ref, own_ref, dso_ref, loc_ref):
    kv_heads, n_rows, dim = qs_ref.shape
    rows = own_ref.shape[2]
    scale = 1.0 / dim**0.5
    allowed = diagonal(low_ref[0:1, :], rows, n_rows)
    for h in range(kv_heads):
        s = lax.dot_general(own_ref[0, h], qs_ref[h], NT, preferred_element_type=F32)
        dp = lax.dot_general(own_ref[1, h], gs_ref[h], NT, preferred_element_type=F32)
        s = jnp.where(allowed, s, -1e30)
        p = jnp.exp2((s - final_ref[h, 0:1, :]) * (scale * LOG2E)) * final_ref[h, 1:2, :]
        ds = (p * (dp - final_ref[h, 2:3, :])).astype(BF)
        dso_ref[h] = ds
        loc_ref[0, h] = jnp.dot(ds, qs_ref[h], preferred_element_type=F32) * scale
        loc_ref[1, h] = jnp.dot(p.astype(BF), gs_ref[h], preferred_element_type=F32)


def query_part(ds_ref, kw_ref, straight_ref, relayed_ref, dso_ref, own_ref, dq_ref, dq_all, out_buf, sems):
    kv_heads, _, n_rows = ds_ref.shape
    rows, dim = own_ref.shape[2:]
    group = n_rows // rows
    heads = kv_heads * group
    step = 256 // heads
    scale = 1.0 / dim**0.5
    for h in range(kv_heads):
        dq = lax.dot_general(kw_ref[h], ds_ref[h, : 2 * rows, :], TN, preferred_element_type=F32)
        dq = dq + lax.dot_general(straight_ref[0, h] + relayed_ref[0, h], ds_ref[h, 2 * rows :, :], TN, preferred_element_type=F32)
        dq = (dq + lax.dot_general(own_ref[0, h], dso_ref[h], TN, preferred_element_type=F32)) * scale
        for x in range(group):
            dq_all[h * group + x] = dq[:, x * rows : (x + 1) * rows].T.astype(BF)
    turn = to_tokens(heads)
    copies = []
    half = rows * heads // 2
    for ch in range(rows // step):
        block = dq_all[:, ch * step : (ch + 1) * step, :].reshape(256, dim)
        out_buf[ch * 256 : (ch + 1) * 256, :] = pick(turn, block)
        if (ch + 1) * 256 % half == 0:
            at = pl.ds(len(copies) * half, half)
            copies.append(pltpu.make_async_copy(out_buf.at[at, :], dq_ref.at[at, :], sems.at[len(copies)]))
            copies[-1].start()
    for copy in copies:
        copy.wait()


def finish(loc_ref, back_ref, away_ref, dk_ref, dv_ref, buf, sems):
    _, kv_heads, rows, dim = loc_ref.shape
    tok = 256 // kv_heads
    turn = to_tokens(kv_heads)
    copies = []
    for s, out in ((0, dk_ref), (1, dv_ref)):
        for ch in range(rows // tok):
            at = (s, slice(None), slice(ch * tok, (ch + 1) * tok), slice(None))
            total = loc_ref[at] + away_ref[at].astype(F32)
            total = total + back_ref[at].astype(F32)
            buf[s, ch * 256 : (ch + 1) * 256, :] = pick(turn, total.astype(BF).reshape(256, dim))
        copies.append(pltpu.make_async_copy(buf.at[s], out, sems.at[s]))
        copies[-1].start()
    for copy in copies:
        copy.wait()


def body(queries, keys, values, out_grad, lengths):
    rows, heads, dim = queries.shape
    kv_heads = keys.shape[1]
    n_rows = heads // kv_heads * rows
    lead = 3 * rows
    n = lax.axis_size("dp") * lax.axis_size("ctx")
    core = lax.rem(lax.axis_index("ctx"), 2)
    place = jnp.stack([lax.axis_index(AXES) * rows]).astype(jnp.int32)
    shape = jax.ShapeDtypeStruct
    sums = (2, kv_heads, rows, dim)

    def mixed(even, odd):
        steps = [(i, i + (odd if i % 2 else even)) for i in range(n)]
        return [(i, j) for i, j in steps if 0 <= j < n]

    n_ctx = lax.axis_size("ctx")
    relay = [(i + 1, i + 2) for i in range(n_ctx // 2, n, n_ctx // 2)]
    skip = [(i - 1, i + 2) for i in range(n_ctx // 2, n, n_ctx // 2)]
    direct = [x for x in mixed(1, 3) if x not in skip]

    hbm = lambda x: pltpu.with_memory_space_constraint(x, pltpu.HBM)
    k_flat, v_flat = keys.reshape(rows * kv_heads, dim), values.reshape(rows * kv_heads, dim)

    own = pl.pallas_call(
        pack,
        in_specs=[IN_HBM] * 2,
        out_shape=shape(sums, BF),
        out_specs=IN_VMEM,
        scratch_shapes=[pltpu.VMEM((rows * kv_heads, dim), BF)] * 2 + [pltpu.SemaphoreType.DMA((2,))],
        compiler_params=PARAMS,
        name="pack",
    )(hbm(k_flat), hbm(v_flat))

    got = lax.ppermute(own, AXES, mixed(2, 2))
    side = lax.ppermute(own, AXES, direct)
    qs, gs, low, stat = pl.pallas_call(
        prepare,
        in_specs=[IN_SMEM, IN_VMEM, IN_HBM, IN_HBM, IN_VMEM],
        out_shape=[shape((kv_heads, n_rows, dim), BF)] * 2 + [shape((8, n_rows), jnp.int32), shape((kv_heads, 8, n_rows), F32)],
        out_specs=[IN_VMEM] * 4,
        scratch_shapes=[pltpu.VMEM((rows * heads, dim), BF)] * 2 + [pltpu.SemaphoreType.DMA((2,))],
        compiler_params=PARAMS,
        cost_estimate=pl.CostEstimate(flops=1_000_000_000, bytes_accessed=4_000_000, transcendentals=1 << 18),
        name="prepare",
    )(place, lengths.reshape(1, -1), hbm(queries.reshape(rows * heads, dim)), hbm(out_grad.reshape(rows * heads, dim)), own)
    got, qs = lax.optimization_barrier((got, qs))
    pairs = [[2 * i, 2 * i + 1] for i in range(lax.axis_size("ctx") // 2)]
    relayed = lax.ppermute(got, AXES, relay)
    both = lax.all_gather(got, "ctx", axis_index_groups=pairs)

    kw_ab, e_ab, dp_ab, stat = pl.pallas_call(
        attend_two,
        in_specs=[IN_VMEM] * 5,
        out_shape=[shape((kv_heads, 2 * rows, dim), BF), shape((kv_heads, 2 * rows, n_rows), F32)]
        + [shape((kv_heads, 2 * rows, n_rows), F32), shape((kv_heads, 8, n_rows), F32)],
        out_specs=[IN_VMEM] * 4,
        scratch_shapes=[pltpu.VMEM((kv_heads, 2 * rows, dim), BF)],
        compiler_params=PARAMS,
        name="attend_two",
    )(low, stat, qs, gs, both)
    ds, final, away, cross, base = pl.pallas_call(
        attend,
        in_specs=[IN_VMEM] * 8,
        out_shape=[shape((kv_heads, lead, n_rows), BF), shape((kv_heads, 8, n_rows), F32)] + [shape(sums, BF)] * 3,
        out_specs=[IN_VMEM] * 5,
        scratch_shapes=[pltpu.VMEM((kv_heads, lead, n_rows), BF)],
        compiler_params=PARAMS,
        name="attend",
    )(low, stat, qs, gs, e_ab, dp_ab, side, relayed)

    away_got = lax.ppermute(away, AXES, mixed(-3, -1))
    crossed = lax.all_gather(cross, "ctx", axis_index_groups=pairs)
    crossed = lax.dynamic_index_in_dim(crossed, 1 - core, 0, keepdims=False)
    part = (base.astype(F32) + crossed.astype(F32)).astype(BF)
    back = lax.ppermute(part, AXES, mixed(-2, -2))
    part, final, kw_ab = lax.optimization_barrier((part, final, kw_ab))
    dso, loc = pl.pallas_call(
        own_part,
        in_specs=[IN_VMEM] * 5,
        out_shape=[shape((kv_heads, rows, n_rows), BF), shape(sums, F32)],
        out_specs=[IN_VMEM] * 2,
        compiler_params=PARAMS,
        cost_estimate=pl.CostEstimate(flops=300_000_000, bytes_accessed=4_000_000, transcendentals=1 << 18),
        name="own_part",
    )(low, final, qs, gs, own)
    dq = pl.pallas_call(
        query_part,
        in_specs=[IN_VMEM] * 6,
        out_shape=shape((rows * heads, dim), BF),
        out_specs=IN_HBM,
        scratch_shapes=[pltpu.VMEM((heads, rows, dim), BF), pltpu.VMEM((rows * heads, dim), BF), pltpu.SemaphoreType.DMA((2,))],
        compiler_params=PARAMS,
        cost_estimate=pl.CostEstimate(flops=800_000_000, bytes_accessed=4_000_000, transcendentals=0),
        name="query_part",
    )(ds, kw_ab, side, relayed, dso, own)

    dk, dv = pl.pallas_call(
        finish,
        in_specs=[IN_VMEM] * 3,
        out_shape=[shape((rows * kv_heads, dim), BF)] * 2,
        out_specs=[IN_HBM] * 2,
        scratch_shapes=[pltpu.VMEM((2, rows * kv_heads, dim), BF), pltpu.SemaphoreType.DMA((2,))],
        compiler_params=PARAMS,
        name="finish",
    )(loc, back, away_got)
    return dq.reshape(rows, heads, dim), dk.reshape(rows, kv_heads, dim), dv.reshape(rows, kv_heads, dim)


def solution(mesh):
    token = P(AXES, None, None)
    return jax.shard_map(
        body,
        mesh=mesh,
        in_specs=(token, token, token, token, P()),
        out_specs=(token, token, token),
        check_vma=False,
    )
```

```python
import jax
import jax.numpy as jnp
from jax import lax
from jax.experimental import pallas as pl
from jax.experimental.pallas import tpu as pltpu
from jax.sharding import PartitionSpec as P

AXES = ("dp", "ctx")
BF = jnp.bfloat16
F32 = jnp.float32
VMEM = 28 * 1024 * 1024
NT = (((1,), (1,)), ((), ()))
TN = (((0,), (0,)), ((), ()))
LOG2E = 1.4426950408889634
PARAMS = pltpu.CompilerParams(vmem_limit_bytes=VMEM)
IN_SMEM = pl.BlockSpec(memory_space=pltpu.SMEM)
IN_VMEM = pl.BlockSpec(memory_space=pltpu.VMEM)
IN_HBM = pl.BlockSpec(memory_space=pltpu.HBM)


def hot(source):
    o = lax.broadcasted_iota(jnp.int32, (256, 256), 0)
    r = lax.broadcasted_iota(jnp.int32, (256, 256), 1)
    return jnp.where(r == source(o), 1.0, 0.0).astype(BF)


def pick(onehot, block):
    return jnp.dot(onehot, block, preferred_element_type=F32).astype(BF)


def to_heads(heads):
    step = 256 // heads
    return hot(lambda o: lax.rem(o, step) * heads + o // step)


def to_tokens(heads):
    step = 256 // heads
    return hot(lambda o: lax.rem(o, heads) * step + o // heads)


def pack(k_ref, v_ref, own_ref, k_buf, v_buf, sems):
    copies = [pltpu.make_async_copy(src, dst, sems.at[i]) for i, (src, dst) in enumerate(((k_ref, k_buf), (v_ref, v_buf)))]
    for copy in copies:
        copy.start()
    _, heads, rows, _ = own_ref.shape
    step = 256 // heads
    turn = to_heads(heads)
    for s, buf in enumerate((k_buf, v_buf)):
        copies[s].wait()
        for ch in range(rows // step):
            got = pick(turn, buf[ch * 256 : (ch + 1) * 256, :])
            for h in range(heads):
                own_ref[s, h, ch * step : (ch + 1) * step, :] = got[h * step : (h + 1) * step, :]


def diagonal(low, rows, n_rows):
    kp = lax.broadcasted_iota(jnp.int32, (rows, n_rows), 0)
    tq = lax.rem(lax.broadcasted_iota(jnp.int32, (1, n_rows), 1), rows)
    return (kp + 3 * rows >= low) & (kp <= tq)


def prepare(place_ref, len_ref, q_ref, g_ref, own_ref, qs_ref, gs_ref, low_ref, stat_ref, q_buf, g_buf, len_buf, sems):
    copies = [pltpu.make_async_copy(src, dst, sems.at[i]) for i, (src, dst) in enumerate(((q_ref, q_buf), (g_ref, g_buf), (len_ref, len_buf)))]
    for copy in copies:
        copy.start()
    kv_heads, n_rows, dim = qs_ref.shape
    rows = own_ref.shape[2]
    group = n_rows // rows
    heads = kv_heads * group
    n_docs = len_ref.shape[0]
    step = 256 // heads
    turn = to_heads(heads)
    start = place_ref[0]
    i = lax.broadcasted_iota(jnp.int32, (n_docs, n_docs), 1)
    j = lax.broadcasted_iota(jnp.int32, (n_docs, n_docs), 0)
    copies[2].wait()
    ends = jnp.sum(jnp.where(i <= j, len_buf[...].reshape(1, n_docs), 0), axis=1, keepdims=True)
    pos = start + lax.rem(lax.broadcasted_iota(jnp.int32, (1, n_rows), 1), rows)
    first = jnp.max(jnp.where(ends <= pos, ends, 0), axis=0, keepdims=True)
    low = first - (start - 3 * rows)
    low_ref[...] = jnp.broadcast_to(low, low_ref.shape)
    for s, (buf, dst) in enumerate(((q_buf, qs_ref), (g_buf, gs_ref))):
        copies[s].wait()
        for ch in range(rows // step):
            got = pick(turn, buf[ch * 256 : (ch + 1) * 256, :])
            for h in range(heads):
                at = (h % group) * rows + ch * step
                dst[h // group, at : at + step, :] = got[h * step : (h + 1) * step, :]
    allowed = diagonal(low, rows, n_rows)
    for h in range(kv_heads):
        s = lax.dot_general(own_ref[0, h], qs_ref[h], NT, preferred_element_type=F32)
        dp = lax.dot_general(own_ref[1, h], gs_ref[h], NT, preferred_element_type=F32)
        s = jnp.where(allowed, s, -1e30)
        top = jnp.max(s, axis=0, keepdims=True)
        e = jnp.exp2((s - top) * (LOG2E / dim**0.5))
        stat_ref[h, 0:1, :] = top
        stat_ref[h, 1:2, :] = jnp.sum(e, axis=0, keepdims=True)
        stat_ref[h, 2:3, :] = jnp.sum(e * dp, axis=0, keepdims=True)


def attend_two(low_ref, stat_ref, qs_ref, gs_ref, both_ref, kw_ref, e_ref, dp_ref, next_ref, vw_buf):
    kv_heads, n_rows, dim = qs_ref.shape
    rows = kw_ref.shape[1] // 2
    core = lax.rem(lax.axis_index(AXES), 2)
    chunk = 256
    for h in range(kv_heads):
        kw_ref[h, :rows, :] = both_ref[core, 0, h]
        kw_ref[h, rows:, :] = both_ref[1 - core, 0, h]
        vw_buf[h, :rows, :] = both_ref[core, 1, h]
        vw_buf[h, rows:, :] = both_ref[1 - core, 1, h]
    kp = lax.broadcasted_iota(jnp.int32, (2 * rows, chunk), 0)
    kp = jnp.where(kp < rows, kp + rows, kp - rows + 2 * rows * (1 - core))
    for h in range(kv_heads):
        for c in range(n_rows // chunk):
            cols = slice(c * chunk, (c + 1) * chunk)
            s = lax.dot_general(kw_ref[h], qs_ref[h, cols, :], NT, preferred_element_type=F32)
            dp = lax.dot_general(vw_buf[h], gs_ref[h, cols, :], NT, preferred_element_type=F32)
            s = jnp.where(kp >= low_ref[0:1, cols], s, -1e30)
            old = stat_ref[h, 0:1, cols]
            top = jnp.maximum(jnp.max(s, axis=0, keepdims=True), old)
            e = jnp.exp2((s - top) * (LOG2E / dim**0.5))
            keep = jnp.exp2((old - top) * (LOG2E / dim**0.5))
            e_ref[h, :, cols] = e
            dp_ref[h, :, cols] = dp
            next_ref[h, 0:1, cols] = top
            next_ref[h, 1:2, cols] = jnp.sum(e, axis=0, keepdims=True) + keep * stat_ref[h, 1:2, cols]
            next_ref[h, 2:3, cols] = jnp.sum(e * dp, axis=0, keepdims=True) + keep * stat_ref[h, 2:3, cols]


def attend(low_ref, stat_ref, qs_ref, gs_ref, e_ref, dp_ref, straight_ref, relayed_ref,
           ds_ref, final_ref, away_ref, cross_ref, base_ref, ps_buf):
    kv_heads, n_rows, dim = qs_ref.shape
    rows = straight_ref.shape[2]
    two = 2 * rows
    scale = 1.0 / dim**0.5
    chunk = 256
    kp = lax.broadcasted_iota(jnp.int32, (rows, chunk), 0) + two * lax.rem(lax.axis_index(AXES), 2)

    def soft(h):
        keys, vals = straight_ref[0, h] + relayed_ref[0, h], straight_ref[1, h] + relayed_ref[1, h]
        for c in range(n_rows // chunk):
            cols = slice(c * chunk, (c + 1) * chunk)
            s = lax.dot_general(keys, qs_ref[h, cols, :], NT, preferred_element_type=F32)
            dp = lax.dot_general(vals, gs_ref[h, cols, :], NT, preferred_element_type=F32)
            s = jnp.where(kp >= low_ref[0:1, cols], s, -1e30)
            old = stat_ref[h, 0:1, cols]
            top = jnp.maximum(jnp.max(s, axis=0, keepdims=True), old)
            e = jnp.exp2((s - top) * (scale * LOG2E))
            keep = jnp.exp2((old - top) * (scale * LOG2E))
            r = 1.0 / (jnp.sum(e, axis=0, keepdims=True) + keep * stat_ref[h, 1:2, cols])
            delta = (jnp.sum(e * dp, axis=0, keepdims=True) + keep * stat_ref[h, 2:3, cols]) * r
            final_ref[h, 0:1, cols] = top
            final_ref[h, 1:2, cols] = r
            final_ref[h, 2:3, cols] = delta
            p = e * r
            ps_buf[h, two:, cols] = p.astype(BF)
            ds_ref[h, two:, cols] = (p * (dp - delta)).astype(BF)
            p = e_ref[h, :, cols] * (keep * r)
            ps_buf[h, :two, cols] = p.astype(BF)
            ds_ref[h, :two, cols] = (p * (dp_ref[h, :, cols] - delta)).astype(BF)

    def sums(h):
        dk = (jnp.dot(ds_ref[h], qs_ref[h], preferred_element_type=F32) * scale).astype(BF)
        dv = jnp.dot(ps_buf[h], gs_ref[h], preferred_element_type=F32).astype(BF)
        for s, x in ((0, dk), (1, dv)):
            base_ref[s, h] = x[:rows]
            cross_ref[s, h] = x[rows:two]
            away_ref[s, h] = x[two:]

    for h in range(kv_heads):
        soft(h)
        if h:
            sums(h - 1)
    sums(kv_heads - 1)


def own_part(low_ref, final_ref, qs_ref, gs_ref, own_ref, dso_ref, loc_ref):
    kv_heads, n_rows, dim = qs_ref.shape
    rows = own_ref.shape[2]
    scale = 1.0 / dim**0.5
    allowed = diagonal(low_ref[0:1, :], rows, n_rows)
    for h in range(kv_heads):
        s = lax.dot_general(own_ref[0, h], qs_ref[h], NT, preferred_element_type=F32)
        dp = lax.dot_general(own_ref[1, h], gs_ref[h], NT, preferred_element_type=F32)
        s = jnp.where(allowed, s, -1e30)
        p = jnp.exp2((s - final_ref[h, 0:1, :]) * (scale * LOG2E)) * final_ref[h, 1:2, :]
        ds = (p * (dp - final_ref[h, 2:3, :])).astype(BF)
        dso_ref[h] = ds
        loc_ref[0, h] = jnp.dot(ds, qs_ref[h], preferred_element_type=F32) * scale
        loc_ref[1, h] = jnp.dot(p.astype(BF), gs_ref[h], preferred_element_type=F32)


def query_part(ds_ref, kw_ref, straight_ref, relayed_ref, dso_ref, own_ref, dq_ref, dq_all, out_buf, sems):
    kv_heads, _, n_rows = ds_ref.shape
    rows, dim = own_ref.shape[2:]
    group = n_rows // rows
    heads = kv_heads * group
    step = 256 // heads
    scale = 1.0 / dim**0.5
    for h in range(kv_heads):
        dq = lax.dot_general(kw_ref[h], ds_ref[h, : 2 * rows, :], TN, preferred_element_type=F32)
        dq = dq + lax.dot_general(straight_ref[0, h] + relayed_ref[0, h], ds_ref[h, 2 * rows :, :], TN, preferred_element_type=F32)
        dq = (dq + lax.dot_general(own_ref[0, h], dso_ref[h], TN, preferred_element_type=F32)) * scale
        for x in range(group):
            dq_all[h * group + x] = dq[:, x * rows : (x + 1) * rows].T.astype(BF)
    turn = to_tokens(heads)
    copies = []
    half = rows * heads // 2
    for ch in range(rows // step):
        block = dq_all[:, ch * step : (ch + 1) * step, :].reshape(256, dim)
        out_buf[ch * 256 : (ch + 1) * 256, :] = pick(turn, block)
        if (ch + 1) * 256 % half == 0:
            at = pl.ds(len(copies) * half, half)
            copies.append(pltpu.make_async_copy(out_buf.at[at, :], dq_ref.at[at, :], sems.at[len(copies)]))
            copies[-1].start()
    for copy in copies:
        copy.wait()


def finish(loc_ref, back_ref, away_ref, dk_ref, dv_ref, buf, sems):
    _, kv_heads, rows, dim = loc_ref.shape
    tok = 256 // kv_heads
    turn = to_tokens(kv_heads)
    copies = []
    for s, out in ((0, dk_ref), (1, dv_ref)):
        for ch in range(rows // tok):
            at = (s, slice(None), slice(ch * tok, (ch + 1) * tok), slice(None))
            total = loc_ref[at] + away_ref[at].astype(F32)
            total = total + back_ref[at].astype(F32)
            buf[s, ch * 256 : (ch + 1) * 256, :] = pick(turn, total.astype(BF).reshape(256, dim))
        copies.append(pltpu.make_async_copy(buf.at[s], out, sems.at[s]))
        copies[-1].start()
    for copy in copies:
        copy.wait()


def body(queries, keys, values, out_grad, lengths):
    rows, heads, dim = queries.shape
    kv_heads = keys.shape[1]
    n_rows = heads // kv_heads * rows
    lead = 3 * rows
    n = lax.axis_size("dp") * lax.axis_size("ctx")
    core = lax.rem(lax.axis_index("ctx"), 2)
    place = jnp.stack([lax.axis_index(AXES) * rows]).astype(jnp.int32)
    shape = jax.ShapeDtypeStruct
    sums = (2, kv_heads, rows, dim)

    def mixed(even, odd):
        steps = [(i, i + (odd if i % 2 else even)) for i in range(n)]
        return [(i, j) for i, j in steps if 0 <= j < n]

    n_ctx = lax.axis_size("ctx")
    relay = [(i + 1, i + 2) for i in range(n_ctx // 2, n, n_ctx // 2)]
    skip = [(i - 1, i + 2) for i in range(n_ctx // 2, n, n_ctx // 2)]
    direct = [x for x in mixed(1, 3) if x not in skip]

    hbm = lambda x: pltpu.with_memory_space_constraint(x, pltpu.HBM)
    k_flat, v_flat = keys.reshape(rows * kv_heads, dim), values.reshape(rows * kv_heads, dim)

    own = pl.pallas_call(
        pack,
        in_specs=[IN_HBM] * 2,
        out_shape=shape(sums, BF),
        out_specs=IN_VMEM,
        scratch_shapes=[pltpu.VMEM((rows * kv_heads, dim), BF)] * 2 + [pltpu.SemaphoreType.DMA((2,))],
        compiler_params=PARAMS,
        name="pack",
    )(hbm(k_flat), hbm(v_flat))

    got = lax.ppermute(own, AXES, mixed(2, 2))
    side = lax.ppermute(own, AXES, direct)
    qs, gs, low, stat = pl.pallas_call(
        prepare,
        in_specs=[IN_SMEM, IN_HBM, IN_HBM, IN_HBM, IN_VMEM],
        out_shape=[shape((kv_heads, n_rows, dim), BF)] * 2 + [shape((8, n_rows), jnp.int32), shape((kv_heads, 8, n_rows), F32)],
        out_specs=[IN_VMEM] * 4,
        scratch_shapes=[pltpu.VMEM((rows * heads, dim), BF)] * 2 + [pltpu.VMEM(lengths.shape, jnp.int32), pltpu.SemaphoreType.DMA((3,))],
        compiler_params=PARAMS,
        cost_estimate=pl.CostEstimate(flops=1_000_000_000, bytes_accessed=4_000_000, transcendentals=1 << 18),
        name="prepare",
    )(place, hbm(lengths), hbm(queries.reshape(rows * heads, dim)), hbm(out_grad.reshape(rows * heads, dim)), own)
    got, qs = lax.optimization_barrier((got, qs))
    pairs = [[2 * i, 2 * i + 1] for i in range(lax.axis_size("ctx") // 2)]
    relayed = lax.ppermute(got, AXES, relay)
    both = lax.all_gather(got, "ctx", axis_index_groups=pairs)

    kw_ab, e_ab, dp_ab, stat = pl.pallas_call(
        attend_two,
        in_specs=[IN_VMEM] * 5,
        out_shape=[shape((kv_heads, 2 * rows, dim), BF), shape((kv_heads, 2 * rows, n_rows), F32)]
        + [shape((kv_heads, 2 * rows, n_rows), F32), shape((kv_heads, 8, n_rows), F32)],
        out_specs=[IN_VMEM] * 4,
        scratch_shapes=[pltpu.VMEM((kv_heads, 2 * rows, dim), BF)],
        compiler_params=PARAMS,
        name="attend_two",
    )(low, stat, qs, gs, both)
    ds, final, away, cross, base = pl.pallas_call(
        attend,
        in_specs=[IN_VMEM] * 8,
        out_shape=[shape((kv_heads, lead, n_rows), BF), shape((kv_heads, 8, n_rows), F32)] + [shape(sums, BF)] * 3,
        out_specs=[IN_VMEM] * 5,
        scratch_shapes=[pltpu.VMEM((kv_heads, lead, n_rows), BF)],
        compiler_params=PARAMS,
        name="attend",
    )(low, stat, qs, gs, e_ab, dp_ab, side, relayed)

    away_got = lax.ppermute(away, AXES, mixed(-3, -1))
    crossed = lax.all_gather(cross, "ctx", axis_index_groups=pairs)
    crossed = lax.dynamic_index_in_dim(crossed, 1 - core, 0, keepdims=False)
    part = (base.astype(F32) + crossed.astype(F32)).astype(BF)
    back = lax.ppermute(part, AXES, mixed(-2, -2))
    part, final, kw_ab = lax.optimization_barrier((part, final, kw_ab))
    dso, loc = pl.pallas_call(
        own_part,
        in_specs=[IN_VMEM] * 5,
        out_shape=[shape((kv_heads, rows, n_rows), BF), shape(sums, F32)],
        out_specs=[IN_VMEM] * 2,
        compiler_params=PARAMS,
        cost_estimate=pl.CostEstimate(flops=300_000_000, bytes_accessed=4_000_000, transcendentals=1 << 18),
        name="own_part",
    )(low, final, qs, gs, own)
    dq = pl.pallas_call(
        query_part,
        in_specs=[IN_VMEM] * 6,
        out_shape=shape((rows * heads, dim), BF),
        out_specs=IN_HBM,
        scratch_shapes=[pltpu.VMEM((heads, rows, dim), BF), pltpu.VMEM((rows * heads, dim), BF), pltpu.SemaphoreType.DMA((2,))],
        compiler_params=PARAMS,
        cost_estimate=pl.CostEstimate(flops=800_000_000, bytes_accessed=4_000_000, transcendentals=0),
        name="query_part",
    )(ds, kw_ab, side, relayed, dso, own)

    dk, dv = pl.pallas_call(
        finish,
        in_specs=[IN_VMEM] * 3,
        out_shape=[shape((rows * kv_heads, dim), BF)] * 2,
        out_specs=[IN_HBM] * 2,
        scratch_shapes=[pltpu.VMEM((2, rows * kv_heads, dim), BF), pltpu.SemaphoreType.DMA((2,))],
        compiler_params=PARAMS,
        name="finish",
    )(loc, back, away_got)
    return dq.reshape(rows, heads, dim), dk.reshape(rows, kv_heads, dim), dv.reshape(rows, kv_heads, dim)


def solution(mesh):
    token = P(AXES, None, None)
    return jax.shard_map(
        body,
        mesh=mesh,
        in_specs=(token, token, token, token, P()),
        out_specs=(token, token, token),
        check_vma=False,
    )
```

```python
import jax
import jax.numpy as jnp
from jax import lax
from jax.experimental import pallas as pl
from jax.experimental.pallas import tpu as pltpu
from jax.sharding import PartitionSpec as P

AXES = ("dp", "ctx")
BF = jnp.bfloat16
F32 = jnp.float32
VMEM = 28 * 1024 * 1024
NT = (((1,), (1,)), ((), ()))
TN = (((0,), (0,)), ((), ()))
LOG2E = 1.4426950408889634
PARAMS = pltpu.CompilerParams(vmem_limit_bytes=VMEM)
IN_SMEM = pl.BlockSpec(memory_space=pltpu.SMEM)
IN_VMEM = pl.BlockSpec(memory_space=pltpu.VMEM)
IN_HBM = pl.BlockSpec(memory_space=pltpu.HBM)


def hot(source):
    o = lax.broadcasted_iota(jnp.int32, (256, 256), 0)
    r = lax.broadcasted_iota(jnp.int32, (256, 256), 1)
    return jnp.where(r == source(o), 1.0, 0.0).astype(BF)


def pick(onehot, block):
    return jnp.dot(onehot, block, preferred_element_type=F32).astype(BF)


def to_heads(heads):
    step = 256 // heads
    return hot(lambda o: lax.rem(o, step) * heads + o // step)


def to_tokens(heads):
    step = 256 // heads
    return hot(lambda o: lax.rem(o, heads) * step + o // heads)


def pack(k_ref, v_ref, own_ref, k_buf, v_buf, sems):
    copies = [pltpu.make_async_copy(src, dst, sems.at[i]) for i, (src, dst) in enumerate(((k_ref, k_buf), (v_ref, v_buf)))]
    for copy in copies:
        copy.start()
    _, heads, rows, _ = own_ref.shape
    step = 256 // heads
    turn = to_heads(heads)
    dim = own_ref.shape[3]
    for copy in copies:
        copy.wait()
    for ch in range(rows // step):
        at = slice(ch * 256, (ch + 1) * 256)
        got = pick(turn, jnp.concatenate([k_buf[at, :], v_buf[at, :]], axis=1))
        for h in range(heads):
            for s in range(2):
                own_ref[s, h, ch * step : (ch + 1) * step, :] = got[h * step : (h + 1) * step, s * dim : (s + 1) * dim]


def diagonal(low, rows, n_rows):
    kp = lax.broadcasted_iota(jnp.int32, (rows, n_rows), 0)
    tq = lax.rem(lax.broadcasted_iota(jnp.int32, (1, n_rows), 1), rows)
    return (kp + 3 * rows >= low) & (kp <= tq)


def prepare(place_ref, len_ref, q_ref, g_ref, own_ref, qs_ref, gs_ref, low_ref, stat_ref, q_buf, g_buf, len_buf, sems):
    copies = [pltpu.make_async_copy(src, dst, sems.at[i]) for i, (src, dst) in enumerate(((q_ref, q_buf), (g_ref, g_buf), (len_ref, len_buf)))]
    for copy in copies:
        copy.start()
    kv_heads, n_rows, dim = qs_ref.shape
    rows = own_ref.shape[2]
    group = n_rows // rows
    heads = kv_heads * group
    n_docs = len_ref.shape[0]
    step = 256 // heads
    turn = to_heads(heads)
    start = place_ref[0]
    i = lax.broadcasted_iota(jnp.int32, (n_docs, n_docs), 1)
    j = lax.broadcasted_iota(jnp.int32, (n_docs, n_docs), 0)
    copies[2].wait()
    ends = jnp.sum(jnp.where(i <= j, len_buf[...].reshape(1, n_docs), 0), axis=1, keepdims=True)
    pos = start + lax.rem(lax.broadcasted_iota(jnp.int32, (1, n_rows), 1), rows)
    first = jnp.max(jnp.where(ends <= pos, ends, 0), axis=0, keepdims=True)
    low = first - (start - 3 * rows)
    low_ref[...] = jnp.broadcast_to(low, low_ref.shape)
    for s, (buf, dst) in enumerate(((q_buf, qs_ref), (g_buf, gs_ref))):
        copies[s].wait()
        for ch in range(rows // step):
            got = pick(turn, buf[ch * 256 : (ch + 1) * 256, :])
            for h in range(heads):
                at = (h % group) * rows + ch * step
                dst[h // group, at : at + step, :] = got[h * step : (h + 1) * step, :]
    allowed = diagonal(low, rows, n_rows)
    for h in range(kv_heads):
        s = lax.dot_general(own_ref[0, h], qs_ref[h], NT, preferred_element_type=F32)
        dp = lax.dot_general(own_ref[1, h], gs_ref[h], NT, preferred_element_type=F32)
        s = jnp.where(allowed, s, -1e30)
        top = jnp.max(s, axis=0, keepdims=True)
        e = jnp.exp2((s - top) * (LOG2E / dim**0.5))
        stat_ref[h, 0:1, :] = top
        stat_ref[h, 1:2, :] = jnp.sum(e, axis=0, keepdims=True)
        stat_ref[h, 2:3, :] = jnp.sum(e * dp, axis=0, keepdims=True)


def attend_two(low_ref, stat_ref, qs_ref, gs_ref, both_ref, kw_ref, e_ref, dp_ref, next_ref, vw_buf):
    kv_heads, n_rows, dim = qs_ref.shape
    rows = kw_ref.shape[1] // 2
    core = lax.rem(lax.axis_index(AXES), 2)
    chunk = 256
    for h in range(kv_heads):
        kw_ref[h, :rows, :] = both_ref[core, 0, h]
        kw_ref[h, rows:, :] = both_ref[1 - core, 0, h]
        vw_buf[h, :rows, :] = both_ref[core, 1, h]
        vw_buf[h, rows:, :] = both_ref[1 - core, 1, h]
    kp = lax.broadcasted_iota(jnp.int32, (2 * rows, chunk), 0)
    kp = jnp.where(kp < rows, kp + rows, kp - rows + 2 * rows * (1 - core))
    for h in range(kv_heads):
        for c in range(n_rows // chunk):
            cols = slice(c * chunk, (c + 1) * chunk)
            s = lax.dot_general(kw_ref[h], qs_ref[h, cols, :], NT, preferred_element_type=F32)
            dp = lax.dot_general(vw_buf[h], gs_ref[h, cols, :], NT, preferred_element_type=F32)
            s = jnp.where(kp >= low_ref[0:1, cols], s, -1e30)
            old = stat_ref[h, 0:1, cols]
            top = jnp.maximum(jnp.max(s, axis=0, keepdims=True), old)
            e = jnp.exp2((s - top) * (LOG2E / dim**0.5))
            keep = jnp.exp2((old - top) * (LOG2E / dim**0.5))
            e_ref[h, :, cols] = e
            dp_ref[h, :, cols] = dp
            next_ref[h, 0:1, cols] = top
            next_ref[h, 1:2, cols] = jnp.sum(e, axis=0, keepdims=True) + keep * stat_ref[h, 1:2, cols]
            next_ref[h, 2:3, cols] = jnp.sum(e * dp, axis=0, keepdims=True) + keep * stat_ref[h, 2:3, cols]


def attend(low_ref, stat_ref, qs_ref, gs_ref, e_ref, dp_ref, straight_ref, relayed_ref,
           ds_ref, final_ref, away_ref, cross_ref, base_ref, ps_buf):
    kv_heads, n_rows, dim = qs_ref.shape
    rows = straight_ref.shape[2]
    two = 2 * rows
    scale = 1.0 / dim**0.5
    chunk = 256
    kp = lax.broadcasted_iota(jnp.int32, (rows, chunk), 0) + two * lax.rem(lax.axis_index(AXES), 2)

    def soft(h):
        keys, vals = straight_ref[0, h] + relayed_ref[0, h], straight_ref[1, h] + relayed_ref[1, h]
        for c in range(n_rows // chunk):
            cols = slice(c * chunk, (c + 1) * chunk)
            s = lax.dot_general(keys, qs_ref[h, cols, :], NT, preferred_element_type=F32)
            dp = lax.dot_general(vals, gs_ref[h, cols, :], NT, preferred_element_type=F32)
            s = jnp.where(kp >= low_ref[0:1, cols], s, -1e30)
            old = stat_ref[h, 0:1, cols]
            top = jnp.maximum(jnp.max(s, axis=0, keepdims=True), old)
            e = jnp.exp2((s - top) * (scale * LOG2E))
            keep = jnp.exp2((old - top) * (scale * LOG2E))
            r = 1.0 / (jnp.sum(e, axis=0, keepdims=True) + keep * stat_ref[h, 1:2, cols])
            delta = (jnp.sum(e * dp, axis=0, keepdims=True) + keep * stat_ref[h, 2:3, cols]) * r
            final_ref[h, 0:1, cols] = top
            final_ref[h, 1:2, cols] = r
            final_ref[h, 2:3, cols] = delta
            p = e * r
            ps_buf[h, two:, cols] = p.astype(BF)
            ds_ref[h, two:, cols] = (p * (dp - delta)).astype(BF)
            p = e_ref[h, :, cols] * (keep * r)
            ps_buf[h, :two, cols] = p.astype(BF)
            ds_ref[h, :two, cols] = (p * (dp_ref[h, :, cols] - delta)).astype(BF)

    def sums(h):
        dk = (jnp.dot(ds_ref[h], qs_ref[h], preferred_element_type=F32) * scale).astype(BF)
        dv = jnp.dot(ps_buf[h], gs_ref[h], preferred_element_type=F32).astype(BF)
        for s, x in ((0, dk), (1, dv)):
            base_ref[s, h] = x[:rows]
            cross_ref[s, h] = x[rows:two]
            away_ref[s, h] = x[two:]

    for h in range(kv_heads):
        soft(h)
        if h:
            sums(h - 1)
    sums(kv_heads - 1)


def own_part(low_ref, final_ref, qs_ref, gs_ref, own_ref, dso_ref, loc_ref):
    kv_heads, n_rows, dim = qs_ref.shape
    rows = own_ref.shape[2]
    scale = 1.0 / dim**0.5
    allowed = diagonal(low_ref[0:1, :], rows, n_rows)
    for h in range(kv_heads):
        s = lax.dot_general(own_ref[0, h], qs_ref[h], NT, preferred_element_type=F32)
        dp = lax.dot_general(own_ref[1, h], gs_ref[h], NT, preferred_element_type=F32)
        s = jnp.where(allowed, s, -1e30)
        p = jnp.exp2((s - final_ref[h, 0:1, :]) * (scale * LOG2E)) * final_ref[h, 1:2, :]
        ds = (p * (dp - final_ref[h, 2:3, :])).astype(BF)
        dso_ref[h] = ds
        loc_ref[0, h] = jnp.dot(ds, qs_ref[h], preferred_element_type=F32) * scale
        loc_ref[1, h] = jnp.dot(p.astype(BF), gs_ref[h], preferred_element_type=F32)


def query_part(ds_ref, kw_ref, straight_ref, relayed_ref, dso_ref, own_ref, dq_ref, dq_all, out_buf, sems):
    kv_heads, _, n_rows = ds_ref.shape
    rows, dim = own_ref.shape[2:]
    group = n_rows // rows
    heads = kv_heads * group
    step = 256 // heads
    scale = 1.0 / dim**0.5
    for h in range(kv_heads):
        dq = lax.dot_general(kw_ref[h], ds_ref[h, : 2 * rows, :], TN, preferred_element_type=F32)
        dq = dq + lax.dot_general(straight_ref[0, h] + relayed_ref[0, h], ds_ref[h, 2 * rows :, :], TN, preferred_element_type=F32)
        dq = (dq + lax.dot_general(own_ref[0, h], dso_ref[h], TN, preferred_element_type=F32)) * scale
        for x in range(group):
            dq_all[h * group + x] = dq[:, x * rows : (x + 1) * rows].T.astype(BF)
    turn = to_tokens(heads)
    copies = []
    half = rows * heads // 2
    for ch in range(rows // step):
        block = dq_all[:, ch * step : (ch + 1) * step, :].reshape(256, dim)
        out_buf[ch * 256 : (ch + 1) * 256, :] = pick(turn, block)
        if (ch + 1) * 256 % half == 0:
            at = pl.ds(len(copies) * half, half)
            copies.append(pltpu.make_async_copy(out_buf.at[at, :], dq_ref.at[at, :], sems.at[len(copies)]))
            copies[-1].start()
    for copy in copies:
        copy.wait()


def finish(loc_ref, back_ref, away_ref, dk_ref, dv_ref, buf, sems):
    _, kv_heads, rows, dim = loc_ref.shape
    tok = 256 // kv_heads
    turn = to_tokens(kv_heads)
    for ch in range(rows // tok):
        both = []
        for s in range(2):
            at = (s, slice(None), slice(ch * tok, (ch + 1) * tok), slice(None))
            total = loc_ref[at] + away_ref[at].astype(F32) + back_ref[at].astype(F32)
            both.append(total.astype(BF).reshape(256, dim))
        got = pick(turn, jnp.concatenate(both, axis=1))
        for s in range(2):
            buf[s, ch * 256 : (ch + 1) * 256, :] = got[:, s * dim : (s + 1) * dim]
    copies = [pltpu.make_async_copy(buf.at[s], out, sems.at[s]) for s, out in ((0, dk_ref), (1, dv_ref))]
    for copy in copies:
        copy.start()
    for copy in copies:
        copy.wait()


def body(queries, keys, values, out_grad, lengths):
    rows, heads, dim = queries.shape
    kv_heads = keys.shape[1]
    n_rows = heads // kv_heads * rows
    lead = 3 * rows
    n = lax.axis_size("dp") * lax.axis_size("ctx")
    core = lax.rem(lax.axis_index("ctx"), 2)
    place = jnp.stack([lax.axis_index(AXES) * rows]).astype(jnp.int32)
    shape = jax.ShapeDtypeStruct
    sums = (2, kv_heads, rows, dim)

    def mixed(even, odd):
        steps = [(i, i + (odd if i % 2 else even)) for i in range(n)]
        return [(i, j) for i, j in steps if 0 <= j < n]

    n_ctx = lax.axis_size("ctx")
    relay = [(i + 1, i + 2) for i in range(n_ctx // 2, n, n_ctx // 2)]
    skip = [(i - 1, i + 2) for i in range(n_ctx // 2, n, n_ctx // 2)]
    direct = [x for x in mixed(1, 3) if x not in skip]

    hbm = lambda x: pltpu.with_memory_space_constraint(x, pltpu.HBM)
    k_flat, v_flat = keys.reshape(rows * kv_heads, dim), values.reshape(rows * kv_heads, dim)

    own = pl.pallas_call(
        pack,
        in_specs=[IN_HBM] * 2,
        out_shape=shape(sums, BF),
        out_specs=IN_VMEM,
        scratch_shapes=[pltpu.VMEM((rows * kv_heads, dim), BF)] * 2 + [pltpu.SemaphoreType.DMA((2,))],
        compiler_params=PARAMS,
        name="pack",
    )(hbm(k_flat), hbm(v_flat))

    got = lax.ppermute(own, AXES, mixed(2, 2))
    side = lax.ppermute(own, AXES, direct)
    qs, gs, low, stat = pl.pallas_call(
        prepare,
        in_specs=[IN_SMEM, IN_HBM, IN_HBM, IN_HBM, IN_VMEM],
        out_shape=[shape((kv_heads, n_rows, dim), BF)] * 2 + [shape((8, n_rows), jnp.int32), shape((kv_heads, 8, n_rows), F32)],
        out_specs=[IN_VMEM] * 4,
        scratch_shapes=[pltpu.VMEM((rows * heads, dim), BF)] * 2 + [pltpu.VMEM(lengths.shape, jnp.int32), pltpu.SemaphoreType.DMA((3,))],
        compiler_params=PARAMS,
        cost_estimate=pl.CostEstimate(flops=1_000_000_000, bytes_accessed=4_000_000, transcendentals=1 << 18),
        name="prepare",
    )(place, hbm(lengths), hbm(queries.reshape(rows * heads, dim)), hbm(out_grad.reshape(rows * heads, dim)), own)
    got, qs = lax.optimization_barrier((got, qs))
    pairs = [[2 * i, 2 * i + 1] for i in range(lax.axis_size("ctx") // 2)]
    relayed = lax.ppermute(got, AXES, relay)
    both = lax.all_gather(got, "ctx", axis_index_groups=pairs)

    kw_ab, e_ab, dp_ab, stat = pl.pallas_call(
        attend_two,
        in_specs=[IN_VMEM] * 5,
        out_shape=[shape((kv_heads, 2 * rows, dim), BF), shape((kv_heads, 2 * rows, n_rows), F32)]
        + [shape((kv_heads, 2 * rows, n_rows), F32), shape((kv_heads, 8, n_rows), F32)],
        out_specs=[IN_VMEM] * 4,
        scratch_shapes=[pltpu.VMEM((kv_heads, 2 * rows, dim), BF)],
        compiler_params=PARAMS,
        name="attend_two",
    )(low, stat, qs, gs, both)
    ds, final, away, cross, base = pl.pallas_call(
        attend,
        in_specs=[IN_VMEM] * 8,
        out_shape=[shape((kv_heads, lead, n_rows), BF), shape((kv_heads, 8, n_rows), F32)] + [shape(sums, BF)] * 3,
        out_specs=[IN_VMEM] * 5,
        scratch_shapes=[pltpu.VMEM((kv_heads, lead, n_rows), BF)],
        compiler_params=PARAMS,
        name="attend",
    )(low, stat, qs, gs, e_ab, dp_ab, side, relayed)

    away_got = lax.ppermute(away, AXES, mixed(-3, -1))
    crossed = lax.all_gather(cross, "ctx", axis_index_groups=pairs)
    crossed = lax.dynamic_index_in_dim(crossed, 1 - core, 0, keepdims=False)
    part = (base.astype(F32) + crossed.astype(F32)).astype(BF)
    back = lax.ppermute(part, AXES, mixed(-2, -2))
    part, final, kw_ab = lax.optimization_barrier((part, final, kw_ab))
    dso, loc = pl.pallas_call(
        own_part,
        in_specs=[IN_VMEM] * 5,
        out_shape=[shape((kv_heads, rows, n_rows), BF), shape(sums, F32)],
        out_specs=[IN_VMEM] * 2,
        compiler_params=PARAMS,
        cost_estimate=pl.CostEstimate(flops=300_000_000, bytes_accessed=4_000_000, transcendentals=1 << 18),
        name="own_part",
    )(low, final, qs, gs, own)
    dq = pl.pallas_call(
        query_part,
        in_specs=[IN_VMEM] * 6,
        out_shape=shape((rows * heads, dim), BF),
        out_specs=IN_HBM,
        scratch_shapes=[pltpu.VMEM((heads, rows, dim), BF), pltpu.VMEM((rows * heads, dim), BF), pltpu.SemaphoreType.DMA((2,))],
        compiler_params=PARAMS,
        cost_estimate=pl.CostEstimate(flops=800_000_000, bytes_accessed=4_000_000, transcendentals=0),
        name="query_part",
    )(ds, kw_ab, side, relayed, dso, own)

    dk, dv = pl.pallas_call(
        finish,
        in_specs=[IN_VMEM] * 3,
        out_shape=[shape((rows * kv_heads, dim), BF)] * 2,
        out_specs=[IN_HBM] * 2,
        scratch_shapes=[pltpu.VMEM((2, rows * kv_heads, dim), BF), pltpu.SemaphoreType.DMA((2,))],
        compiler_params=PARAMS,
        name="finish",
    )(loc, back, away_got)
    return dq.reshape(rows, heads, dim), dk.reshape(rows, kv_heads, dim), dv.reshape(rows, kv_heads, dim)


def solution(mesh):
    token = P(AXES, None, None)
    return jax.shard_map(
        body,
        mesh=mesh,
        in_specs=(token, token, token, token, P()),
        out_specs=(token, token, token),
        check_vma=False,
    )
```
